32 devices in a mesh: section: 8 (over z, core), expert: 4 (over y, x).
Axes of the slice: x: 2, y: 2, z: 4, core: 2. Of those that a mesh axis runs over, the one named last changes fastest.
Arguments:
- left_in: bfloat16 [8, 256, 2048], P('section', 'expert'), may hold values from -6 to 6
- left_new: bfloat16 [256, 2048], P('expert'), may hold values from -6 to 6
- left_saved: bfloat16 [8, 256, 2048], P('section', 'expert'), may hold values from -6 to 6
- left_cot: bfloat16 [8, 256, 2048], P('section', 'expert'), may hold values from -6 to 6
- right_in: bfloat16 [8, 256, 2048], P('section', 'expert'), may hold values from -6 to 6
- right_saved: bfloat16 [2, 8, 256, 2048], P(None, 'section', 'expert'), may hold values from -6 to 6
- right_cot: bfloat16 [8, 256, 2048], P('section', 'expert'), may hold values from -6 to 6
- right_cot_new: bfloat16 [256, 2048], P('expert'), may hold values from -6 to 6
- expert_ids: int32 [3, 2, 8, 256, 1], P(None, None, 'section', 'expert'), may hold values from 0 to 1; in each aligned block of 64 rows (0 to 63, 64 to 127, ..., all dimensions but the last counted through in order) at most 34 rows name the same one
- gate_values: float32 [3, 2, 8, 256, 1], P(None, None, 'section', 'expert'), may hold values from 0.25 to 1
- w_gate: bfloat16 [8, 4, 2048, 384], P('section', 'expert'), may hold values from -0.125 to 0.125
- w_up: bfloat16 [8, 4, 2048, 384], P('section', 'expert'), may hold values from -0.125 to 0.125
- w_down: bfloat16 [8, 4, 384, 2048], P('section', 'expert'), may hold values from -0.21875 to 0.21875
Outputs:
- left_out: bfloat16 [2, 8, 256, 2048], P(None, 'section', 'expert')
- right_out: bfloat16 [8, 256, 2048], P('section', 'expert')
- left_back: bfloat16 [8, 256, 2048], P('section', 'expert')
- right_back: bfloat16 [2, 8, 256, 2048], P(None, 'section', 'expert')
- grad_gate: bfloat16 [8, 4, 2048, 384], P('section', 'expert')
- grad_up: bfloat16 [8, 4, 2048, 384], P('section', 'expert')
- grad_down: bfloat16 [8, 4, 384, 2048], P('section', 'expert')
The draws below stay inside these ranges and needn't reach their ends.
Inputs may be any that keep to these rules, and one draw needn't show every extreme that they name: `expert_ids`: each row names one expert. In each aligned block of 64 rows (one device's tokens in one pass) no expert is named by more than 34 rows, and in some blocks one expert is named by exactly 34 rows.
All inputs are finite; a program needn't handle non-finite values.
Results may differ from the reference program's by a relative error of at most 0.0064.
Values may be sent and summed in bfloat16 or wider, within the bound.
No kernel may reach another device: no remote copies, remote signals or barrier semaphores. Data moves between devices by JAX's collectives and lax.ppermute only.
A program may use at most 128 MiB of HBM per device.

```python
import math
from functools import partial
import jax
import jax.numpy as jnp
import numpy as np
from jax import lax

D = 2048
FF = 768
TOP = 1
SLOTS = 3
TOK_DEV = 64
HALF = 384
EXPERTS = 2
CAP = 34
TOKENS = 256
SECTIONS = 8
N_EXPERT = 4


def level_of(stream_key, dims, shards, smallest, top_value):
    def one(dim, blocks):
        heights = jax.random.uniform(jax.random.fold_in(jax.random.fold_in(stream_key, 6), dim), (blocks,), jnp.float32, smallest / len(shards), top_value / len(shards))
        return jnp.repeat(jnp.exp(heights), dims[dim] // blocks).reshape((-1,) + (1,) * (len(dims) - dim - 1))

    loudness = one(*shards[0])
    for cut in shards[1:]:
        loudness = loudness * one(*cut)
    return loudness


def deal_out(stream_key, own, number, rows, number_of, top, most, lean):
    sequence = jax.random.permutation(stream_key, number_of)
    heavy_load, usual = portions_of(number_of, rows * top, most, lean, True), portions_of(number_of, rows * top, most, lean, False)
    places = jnp.arange(number_of)

    def named(lengths, offset_by):
        used = int((lengths > 0).sum())
        fixed = max(1, used // 4)
        passed = fixed + (places - fixed + offset_by * (used - fixed)) % max(1, number_of - fixed)
        return jnp.zeros((number_of,), jnp.int32).at[sequence[jnp.where(places < fixed, places, passed)]].set(jnp.asarray(lengths, jnp.int32))

    lengths = jnp.where(number % 4 == 0, named(heavy_load, number // 4), named(usual, number - number // 4 - 1))
    mixed = jax.random.permutation(jax.random.fold_in(own, 3), number_of)
    source_of, receiver = mixed[0:number_of // 2 * 2:2], mixed[1:number_of // 2 * 2:2]
    slack = jnp.minimum(lengths[source_of] - 1, most - lengths[receiver]) // 2
    slack = jnp.where((source_of == sequence[0]) | (receiver == sequence[0]) | (lengths[receiver] == 0), 0, jnp.maximum(slack, 0))
    passed = jax.random.randint(jax.random.fold_in(own, 4), (number_of // 2,), 0, 1 << 20) % (slack + 1)
    lengths = lengths.at[source_of].add(-passed).at[receiver].add(passed)
    members = jnp.searchsorted(jnp.cumsum(lengths), jnp.arange(rows * top), side="right").astype(jnp.int32)
    table = members.reshape(top, rows).T
    table = table[jax.random.permutation(jax.random.fold_in(own, 1), rows)]
    offset_by = jax.random.randint(jax.random.fold_in(own, 2), (rows, 1), 0, top)
    return jnp.take_along_axis(table, (jnp.arange(top)[None, :] + offset_by) % top, axis=1)


def portions_of(amount, total, reach, lean, full):
    loads = [(1 << 20) // math.isqrt(standing ** lean) + 1 for standing in range(1, amount + 1)]
    largest = reach if full else min(reach, max(-(-total // amount), total * loads[0] // sum(loads)))
    least = 1 if total - largest >= amount - 1 else 0
    holding, spare = [largest] + [least] * (amount - 1), total - largest - least * (amount - 1)
    while spare > 0:
        movable = [i for i in range(1, amount) if holding[i] < largest] or [i for i in range(1, amount) if holding[i] < reach]
        mass, left = sum([loads[i] for i in movable]), spare
        for i in movable:
            more = min(reach - holding[i], max(1, left * loads[i] // mass), spare)
            holding[i] = holding[i] + more
            spare = spare - more
    return np.array(holding)


def noise(rng, dims, spread, most, split=(), held_as=jnp.bfloat16):
    entries = spread * jax.random.normal(rng, dims, jnp.float32)
    if split:
        entries = entries * level_of(rng, dims, split, -0.22, 0.18)
    return jnp.clip(entries, -most, most).astype(held_as)


def setup_inputs(seed: int = 0) -> dict:
    splits = jax.random.split(jax.random.key(seed), 14)
    left_in = noise(splits[0], (SECTIONS, TOKENS, D), 1.0, 6.0, ((0, 8), (1, 4)))
    left_new = noise(splits[1], (TOKENS, D), 1.0, 6.0, ((0, 4),))
    left_saved = noise(splits[2], (SECTIONS, TOKENS, D), 1.0, 6.0, ((0, 8), (1, 4)))
    left_cot = noise(splits[3], (SECTIONS, TOKENS, D), 1.0, 6.0, ((0, 8), (1, 4)))
    right_in = noise(splits[4], (SECTIONS, TOKENS, D), 1.0, 6.0, ((0, 8), (1, 4)))
    right_saved = noise(splits[5], (2, SECTIONS, TOKENS, D), 1.0, 6.0, ((1, 8), (2, 4)))
    right_cot = noise(splits[6], (SECTIONS, TOKENS, D), 1.0, 6.0, ((0, 8), (1, 4)))
    right_cot_new = noise(splits[7], (TOKENS, D), 1.0, 6.0, ((0, 4),))
    expert_ids_keys = jax.random.split(jax.random.fold_in(splits[8], 1), SLOTS * 2 * SECTIONS * TOKENS // TOK_DEV)
    expert_ids_turns = jax.random.permutation(jax.random.fold_in(splits[8], 3), SLOTS * 2 * SECTIONS * TOKENS // TOK_DEV)
    expert_ids = jax.vmap(lambda own, number: deal_out(jax.random.fold_in(splits[8], 2), own, number, TOK_DEV, EXPERTS, TOP, CAP, 2))(expert_ids_keys, expert_ids_turns).reshape((SLOTS, 2, SECTIONS, TOKENS, TOP))
    gate_values = jnp.clip(0.25 + 0.75 * jax.random.uniform(splits[9], (SLOTS, 2, SECTIONS, TOKENS, TOP), jnp.float32) ** level_of(splits[9], (SLOTS, 2, SECTIONS, TOKENS, TOP), ((2, 8), (3, 4)), -0.2, 0.2), 0.25, 1.0)
    w_gate = noise(splits[10], (SECTIONS, 2 * EXPERTS, D, HALF), D ** -0.5, 0.125, ((0, 8), (1, 4)))
    w_up = noise(splits[11], (SECTIONS, 2 * EXPERTS, D, HALF), D ** -0.5, 0.125, ((0, 8), (1, 4)))
    w_down = noise(splits[12], (SECTIONS, 2 * EXPERTS, HALF, D), FF ** -0.5, 0.21875, ((0, 8), (1, 4)))
    return {"left_in": left_in, "left_new": left_new, "left_saved": left_saved, "left_cot": left_cot, "right_in": right_in, "right_saved": right_saved, "right_cot": right_cot, "right_cot_new": right_cot_new, "expert_ids": expert_ids, "gate_values": gate_values, "w_gate": w_gate, "w_up": w_up, "w_down": w_down}


HIGHEST = lax.Precision.HIGHEST


def route_tables(ids_block, gates_block, experts, capacity):
    token_count = ids_block.shape[0]
    top_count = ids_block.shape[1]
    flat_ids = ids_block.reshape(-1).astype(jnp.int32)
    onehot = (flat_ids[:, None] == jnp.arange(experts, dtype=jnp.int32)[None, :]).astype(jnp.int32)
    before = jnp.cumsum(onehot, axis=0) - onehot
    position = jnp.sum(before * onehot, axis=1)
    target = (flat_ids * capacity + position).reshape(token_count, top_count)
    slot_ids = jnp.arange(experts * capacity, dtype=jnp.int32)
    matches = target[None, :, :] == slot_ids[:, None, None]
    placement = jnp.sum(matches.astype(jnp.float32), axis=2)
    weighting = jnp.sum(jnp.where(matches, gates_block[None, :, :], jnp.zeros_like(gates_block)[None]), axis=2)
    return placement, weighting


def expert_forward(expert_rows, gate_half, up_half, down_half):
    gate_act = jnp.dot(expert_rows, gate_half, preferred_element_type=jnp.float32)
    up_act = jnp.dot(expert_rows, up_half, preferred_element_type=jnp.float32)
    hidden = (gate_act * jax.nn.sigmoid(gate_act) * up_act).astype(jnp.bfloat16)
    return jnp.dot(hidden, down_half, preferred_element_type=jnp.float32)


def expert_backward(expert_rows, row_cot, gate_half, up_half, down_half):
    gate_act = jnp.dot(expert_rows, gate_half, preferred_element_type=jnp.float32)
    up_act = jnp.dot(expert_rows, up_half, preferred_element_type=jnp.float32)
    logistic = jax.nn.sigmoid(gate_act)
    swish = gate_act * logistic
    hidden = (swish * up_act).astype(jnp.bfloat16)
    d_hidden = jnp.dot(row_cot, down_half.T, preferred_element_type=jnp.float32)
    d_gate = (d_hidden * up_act * logistic * (1.0 + gate_act * (1.0 - logistic))).astype(jnp.bfloat16)
    d_up = (d_hidden * swish).astype(jnp.bfloat16)
    grad_down = jnp.dot(hidden.T, row_cot, preferred_element_type=jnp.float32)
    grad_gate = jnp.dot(expert_rows.T, d_gate, preferred_element_type=jnp.float32)
    grad_up = jnp.dot(expert_rows.T, d_up, preferred_element_type=jnp.float32)
    backward_rows = jnp.dot(d_gate, gate_half.T, preferred_element_type=jnp.float32) + jnp.dot(d_up, up_half.T, preferred_element_type=jnp.float32)
    return backward_rows, grad_gate, grad_up, grad_down


def add_halves(lower, upper):
    return (lower.astype(jnp.bfloat16).astype(jnp.float32) + upper.astype(jnp.bfloat16).astype(jnp.float32)).astype(jnp.bfloat16)


def to_experts(routed, experts, capacity):
    blocks = routed.shape[0]
    model_width = routed.shape[2]
    return routed.reshape(blocks, experts, capacity, model_width).transpose(1, 0, 2, 3).reshape(experts, blocks * capacity, model_width)


def to_blocks(routed, blocks, capacity):
    experts = routed.shape[0]
    model_width = routed.shape[2]
    return routed.reshape(experts, blocks, capacity, model_width).transpose(1, 0, 2, 3).reshape(blocks, experts * capacity, model_width)


def section_tables(ids_section, gates_section):
    experts = N_EXPERT // 2
    tables = jax.vmap(partial(route_tables, experts=experts, capacity=CAP))
    return tables(ids_section.reshape(N_EXPERT, TOK_DEV, TOP), gates_section.reshape(N_EXPERT, TOK_DEV, TOP))


def section_forward(operands):
    tokens, ids_section, gates_section, gate_pairs, up_pairs, down_pairs = operands
    experts = N_EXPERT // 2
    model_width = tokens.shape[1]
    token_blocks = tokens.reshape(N_EXPERT, TOK_DEV, model_width)
    placement, weighting = section_tables(ids_section, gates_section)
    routed = jnp.einsum("bst,btd->bsd", placement, token_blocks.astype(jnp.float32), precision=HIGHEST).astype(jnp.bfloat16)
    per_expert = to_experts(routed, experts, CAP)

    def one_expert(expert_operands):
        expert_rows, gate_pair, up_pair, down_pair = expert_operands
        lower = expert_forward(expert_rows, gate_pair[0], up_pair[0], down_pair[0])
        upper = expert_forward(expert_rows, gate_pair[1], up_pair[1], down_pair[1])
        return add_halves(lower, upper)

    outputs = lax.map(one_expert, (per_expert, gate_pairs.reshape(experts, 2, model_width, HALF), up_pairs.reshape(experts, 2, model_width, HALF), down_pairs.reshape(experts, 2, HALF, model_width)))
    by_block = to_blocks(outputs, N_EXPERT, CAP)
    mixed_out = token_blocks.astype(jnp.float32) + jnp.einsum("bst,bsd->btd", weighting, by_block.astype(jnp.float32), precision=HIGHEST)
    return mixed_out.reshape(tokens.shape).astype(jnp.bfloat16)


def section_backward(operands):
    tokens, cotangent, ids_section, gates_section, gate_pairs, up_pairs, down_pairs = operands
    experts = N_EXPERT // 2
    model_width = tokens.shape[1]
    token_blocks = tokens.reshape(N_EXPERT, TOK_DEV, model_width)
    cot_blocks = cotangent.reshape(N_EXPERT, TOK_DEV, model_width)
    placement, weighting = section_tables(ids_section, gates_section)
    routed = jnp.einsum("bst,btd->bsd", placement, token_blocks.astype(jnp.float32), precision=HIGHEST).astype(jnp.bfloat16)
    row_cot = jnp.einsum("bst,btd->bsd", weighting, cot_blocks.astype(jnp.float32), precision=HIGHEST).astype(jnp.bfloat16)

    def one_expert(expert_operands):
        expert_rows, expert_cot, gate_pair, up_pair, down_pair = expert_operands
        lower = expert_backward(expert_rows, expert_cot, gate_pair[0], up_pair[0], down_pair[0])
        upper = expert_backward(expert_rows, expert_cot, gate_pair[1], up_pair[1], down_pair[1])
        summed = add_halves(lower[0], upper[0])
        return summed, jnp.stack([lower[1], upper[1]]), jnp.stack([lower[2], upper[2]]), jnp.stack([lower[3], upper[3]])

    results = lax.map(one_expert, (to_experts(routed, experts, CAP), to_experts(row_cot, experts, CAP), gate_pairs.reshape(experts, 2, model_width, HALF), up_pairs.reshape(experts, 2, model_width, HALF), down_pairs.reshape(experts, 2, HALF, model_width)))
    by_block = to_blocks(results[0], N_EXPERT, CAP)
    new_cot = cot_blocks.astype(jnp.float32) + jnp.einsum("bst,bsd->btd", placement, by_block.astype(jnp.float32), precision=HIGHEST)
    grad_gate = results[1].reshape(2 * experts, model_width, HALF)
    grad_up = results[2].reshape(2 * experts, model_width, HALF)
    grad_down = results[3].reshape(2 * experts, HALF, model_width)
    return new_cot.reshape(cotangent.shape).astype(jnp.bfloat16), grad_gate, grad_up, grad_down


def backward_cot(operands):
    return section_backward(operands)[0]


def three_passes(operands):
    passes, section_weights = operands
    totals = []
    cots = []
    for saved_rows, cot_rows, ids_section, gates_section in passes:
        result = section_backward((saved_rows, cot_rows, ids_section, gates_section) + section_weights)
        cots.append(result[0])
        if len(totals) == 0:
            totals = [result[1], result[2], result[3]]
        else:
            totals = [totals[0] + result[1], totals[1] + result[2], totals[2] + result[3]]
    return cots[1], cots[2], totals[0].astype(jnp.bfloat16), totals[1].astype(jnp.bfloat16), totals[2].astype(jnp.bfloat16)


def reference(left_in, left_new, left_saved, left_cot, right_in, right_saved, right_cot, right_cot_new, expert_ids, gate_values, w_gate, w_up, w_down):
    saved_zero = right_saved[0][::-1]
    saved_two = right_saved[1][::-1]
    cot_zero = right_cot[::-1]
    left_zero = lax.map(section_forward, (left_in, expert_ids[0, 0], gate_values[0, 0], w_gate, w_up, w_down))
    back_zero = lax.map(backward_cot, (saved_zero, cot_zero, expert_ids[0, 1], gate_values[0, 1], w_gate, w_up, w_down))
    right_one = lax.map(section_forward, (right_in[::-1], expert_ids[1, 0], gate_values[1, 0], w_gate, w_up, w_down))
    left_two_in = jnp.concatenate([left_new[None], left_zero[:-1]], axis=0)
    left_two = lax.map(section_forward, (left_two_in, expert_ids[2, 0], gate_values[2, 0], w_gate, w_up, w_down))
    cot_two = jnp.concatenate([back_zero[1:], right_cot_new[None]], axis=0)
    passes = ((saved_zero, cot_zero, expert_ids[0, 1], gate_values[0, 1]), (left_saved, left_cot, expert_ids[1, 1], gate_values[1, 1]), (saved_two, cot_two, expert_ids[2, 1], gate_values[2, 1]))
    back_one, back_two, grad_gate, grad_up, grad_down = lax.map(three_passes, (passes, (w_gate, w_up, w_down)))
    left_out = jnp.stack([left_zero, left_two])
    right_back = jnp.stack([back_zero, back_two])
    return left_out, right_one, back_one, right_back, grad_gate, grad_up, grad_down
```

```python
import functools

import jax
import jax.numpy as jnp
from jax import lax
from jax.experimental import pallas as pl
from jax.experimental.pallas import tpu as pltpu
from jax.sharding import PartitionSpec as P

LANES = 128
F32 = jnp.float32
BF16 = jnp.bfloat16
VMEM_LIMIT = 40 * 1024 * 1024


class Layout:
    def __init__(self, peers, tokens, width):
        self.peers = peers
        self.experts = peers // 2
        self.tokens = tokens
        self.width = width
        self.cap = min(tokens, 2 * ((tokens // self.experts + 1) // 2) + 2)
        self.main = self.cap // 8 * 8
        self.extra = self.cap - self.main
        self.slabs = width // LANES
        self.per_group = self.main // self.extra if self.extra else 1
        self.groups = -(-self.slabs // self.per_group) if self.extra else 0
        self.packed = width + self.groups * LANES
        self.slots = -(-(self.experts * self.cap) // 16) * 16
        self.rows = peers * self.cap
        self.rows_held = -(-self.rows // 16) * 16


def slab_place(lay, slab):
    group, at = divmod(slab, lay.per_group)
    return at * lay.extra, lay.width + group * LANES


def pack_extra(lay, rows, start, out_ref, lead, stage):
    if not lay.extra:
        return
    if lay.slabs % lay.per_group:
        stage[...] = jnp.zeros_like(stage)
    part = rows[start : start + lay.extra, :]
    for slab in range(lay.slabs):
        row, col = slab_place(lay, slab)
        stage[row : row + lay.extra, col - lay.width : col - lay.width + LANES] = part[
            :, slab * LANES : (slab + 1) * LANES
        ]
    out_ref[lead, :, lay.width :] = stage[...].astype(BF16)


def unpack_extra(lay, packed, stage, into, row_at):
    stage[...] = packed
    for slab in range(lay.slabs):
        row, col = slab_place(lay, slab)
        into[row_at : row_at + lay.extra, slab * LANES : (slab + 1) * LANES] = stage[
            row : row + lay.extra, col - lay.width : col - lay.width + LANES
        ]


def stacked_main(lay, blocks):
    if lay.main % 16:
        return jnp.concatenate([b.astype(F32) for b in blocks], axis=0).astype(BF16)
    return jnp.concatenate(blocks, axis=0)


def slot_onehot(lay, ids, own_expert):
    tokens = lay.tokens
    down = lax.broadcasted_iota(jnp.int32, (tokens, tokens), 0)
    across = lax.broadcasted_iota(jnp.int32, (tokens, tokens), 1)
    ids_row = jnp.sum(jnp.where(down == across, ids, 0), axis=0, keepdims=True)
    earlier = jnp.logical_and(ids == ids_row, down < across)
    rank = jnp.sum(earlier.astype(jnp.int32), axis=0, keepdims=True)
    near = ids_row ^ own_expert
    slot = jnp.where(
        rank < lay.main,
        near * lay.main + rank,
        lay.experts * lay.main + near * lay.extra + rank - lay.main,
    )
    place = lax.broadcasted_iota(jnp.int32, (lay.slots, tokens), 0)
    return (place == slot).astype(F32).astype(BF16)


def stage_shape(lay):
    return pltpu.VMEM((lay.main, max(1, lay.groups) * LANES), F32)


def route_kernel(lay, plan, *refs):
    scalars = refs[0]
    at = 1
    items = []
    for has_gates, has_choice in plan:
        item = {"tokens": refs[at], "ids": refs[at + 1]}
        at += 2
        if has_gates:
            item["gates"] = refs[at]
            at += 1
        if has_choice:
            item["fresh"] = refs[at]
            at += 1
        items.append(item)
    outs = refs[at : at + lay.experts]
    stage = refs[at + lay.experts]
    for lead, item in enumerate(items):
        tokens = item["tokens"][...]
        if "fresh" in item:
            tokens = jnp.where(scalars[1] == 1, item["fresh"][...], tokens)
        if "gates" in item:
            tokens = (item["gates"][...] * tokens.astype(F32)).astype(BF16)
        onehot = slot_onehot(lay, item["ids"][...], scalars[0])
        rows = jnp.dot(onehot, tokens, preferred_element_type=F32)
        for j, out in enumerate(outs):
            out[lead, :, : lay.width] = rows[j * lay.main : (j + 1) * lay.main].astype(BF16)
            pack_extra(lay, rows, lay.experts * lay.main + j * lay.extra, out, lead, stage)


VMEM_SPEC = pl.BlockSpec(memory_space=pltpu.VMEM)
SMEM_SPEC = pl.BlockSpec(memory_space=pltpu.SMEM)


def cost(flops, arrays):
    moved = sum(a.size * a.dtype.itemsize for a in arrays)
    return pl.CostEstimate(flops=int(flops), bytes_accessed=int(moved), transcendentals=0)


def call(kernel, args, outs, scratch, flops, smem_first=False):
    specs = [VMEM_SPEC] * len(args)
    if smem_first:
        specs[0] = SMEM_SPEC
    return pl.pallas_call(
        kernel,
        out_shape=outs,
        in_specs=specs,
        out_specs=[VMEM_SPEC] * len(outs),
        scratch_shapes=scratch,
        compiler_params=pltpu.CompilerParams(vmem_limit_bytes=VMEM_LIMIT),
        cost_estimate=cost(flops, list(args) + list(outs)),
    )(*args)


def route(lay, scalars, items):
    args = [scalars]
    plan = []
    for tokens, ids, gates, fresh in items:
        args += [tokens, ids]
        if gates is not None:
            args.append(gates)
        if fresh is not None:
            args.append(fresh)
        plan.append((gates is not None, fresh is not None))
    out = jax.ShapeDtypeStruct((len(items), lay.main, lay.packed), BF16)
    return call(
        functools.partial(route_kernel, lay, tuple(plan)),
        args,
        [out] * lay.experts,
        [stage_shape(lay)],
        2 * lay.slots * lay.tokens * lay.width * len(items),
        smem_first=True,
    )


def exchange(lay, by_distance):
    got = [by_distance[0]]
    for d in range(1, lay.peers):
        pairs = [(i, i ^ d) for i in range(lay.peers)]
        got.append(lax.ppermute(by_distance[d], "expert", pairs))
    return got


def dispatch(lay, payloads):
    return exchange(lay, [payloads[d // 2] for d in range(lay.peers)])


def load_rows(lay, refs, lead, stage, extra_rows):
    main = stacked_main(lay, [r[lead, :, : lay.width] for r in refs])
    if not lay.extra:
        return main
    extra_rows[...] = jnp.zeros_like(extra_rows)
    for d, ref in enumerate(refs):
        unpack_extra(lay, ref[lead, :, lay.width :].astype(F32), stage, extra_rows, d * lay.extra)
    return jnp.concatenate([main, extra_rows[...].astype(BF16)], axis=0)


def store_parts(lay, rows, refs, stage):
    for d, ref in enumerate(refs):
        ref[0, :, : lay.width] = rows[d * lay.main : (d + 1) * lay.main].astype(BF16)
        pack_extra(lay, rows, lay.peers * lay.main + d * lay.extra, ref, 0, stage)


def extra_shape(lay):
    return pltpu.VMEM((lay.rows_held - lay.peers * lay.main, lay.width), F32)


NT = (((1,), (1,)), ((), ()))
TN = (((0,), (0,)), ((), ()))


def forward_kernel(lay, lead, *refs):
    blocks = refs[: lay.peers]
    w_gate, w_up, w_down = refs[lay.peers : lay.peers + 3]
    outs = refs[lay.peers + 3 : 2 * lay.peers + 3]
    stage, extra_rows = refs[2 * lay.peers + 3 :]
    rows = load_rows(lay, blocks, lead, stage, extra_rows)
    gate = jnp.dot(rows, w_gate[...], preferred_element_type=F32)
    up = jnp.dot(rows, w_up[...], preferred_element_type=F32)
    hidden = (gate * jax.nn.sigmoid(gate) * up).astype(BF16)
    part = jnp.dot(hidden, w_down[...], preferred_element_type=F32)
    store_parts(lay, part, outs, stage)


def forward(lay, blocks, lead, weights):
    out = jax.ShapeDtypeStruct((1, lay.main, lay.packed), BF16)
    return call(
        functools.partial(forward_kernel, lay, lead),
        list(blocks) + list(weights),
        [out] * lay.peers,
        [stage_shape(lay), extra_shape(lay)],
        2 * 3 * lay.rows * lay.width * weights[0].shape[1],
    )


def backward_kernel(lay, row_lead, cot_lead, *refs):
    n = lay.peers
    row_blocks, cot_blocks = refs[:n], refs[n : 2 * n]
    w_gate, w_up, w_down = refs[2 * n : 2 * n + 3]
    outs = refs[2 * n + 3 : 3 * n + 3]
    rows_out, cot_out, d_gate_out, d_up_out, hidden_out = refs[3 * n + 3 : 3 * n + 8]
    stage, extra_rows = refs[3 * n + 8 :]
    rows = load_rows(lay, row_blocks, row_lead, stage, extra_rows)
    rows_out[...] = rows
    gate = jnp.dot(rows, w_gate[...], preferred_element_type=F32)
    up = jnp.dot(rows, w_up[...], preferred_element_type=F32)
    row_cot = load_rows(lay, cot_blocks, cot_lead, stage, extra_rows)
    cot_out[...] = row_cot
    d_hidden = lax.dot_general(row_cot, w_down[...], NT, preferred_element_type=F32)
    logistic = jax.nn.sigmoid(gate)
    swish = gate * logistic
    hidden_out[...] = (swish * up).astype(BF16)
    d_gate = (d_hidden * up * logistic * (1.0 + gate * (1.0 - logistic))).astype(BF16)
    d_up = (d_hidden * swish).astype(BF16)
    d_gate_out[...] = d_gate
    d_up_out[...] = d_up
    back = lax.dot_general(d_gate, w_gate[...], NT, preferred_element_type=F32)
    back = back + lax.dot_general(d_up, w_up[...], NT, preferred_element_type=F32)
    store_parts(lay, back, outs, stage)


def backward(lay, rows, row_lead, cots, cot_lead, weights):
    half = weights[0].shape[1]
    out = jax.ShapeDtypeStruct((1, lay.main, lay.packed), BF16)
    wide = jax.ShapeDtypeStruct((lay.rows_held, lay.width), BF16)
    narrow = jax.ShapeDtypeStruct((lay.rows_held, half), BF16)
    got = call(
        functools.partial(backward_kernel, lay, row_lead, cot_lead),
        list(rows) + list(cots) + list(weights),
        [out] * lay.peers + [wide, wide, narrow, narrow, narrow],
        [stage_shape(lay), extra_shape(lay)],
        2 * 5 * lay.rows * lay.width * half,
    )
    return got[: lay.peers], got[lay.peers :]


def combine_kernel(lay, has_gates, has_choice, has_first, *refs):
    scalars, tokens_ref, ids_ref = refs[:3]
    at = 3
    tokens = tokens_ref[...]
    if has_choice:
        tokens = jnp.where(scalars[1] == 1, refs[at][...], tokens)
        at += 1
    if has_gates:
        gates = refs[at][...]
        at += 1
    if has_first:
        first = refs[at]
        at += 1
    parts = refs[at : at + lay.peers]
    out, stage, extra_rows = refs[at + lay.peers :]
    mains = []
    if lay.extra:
        extra_rows[...] = jnp.zeros_like(extra_rows)
    for j in range(lay.experts):
        total = parts[2 * j][0].astype(F32) + parts[2 * j + 1][0].astype(F32)
        mains.append(total[:, : lay.width].astype(BF16))
        if lay.extra:
            unpack_extra(lay, total[:, lay.width :], stage, extra_rows, j * lay.extra)
    outputs = stacked_main(lay, mains)
    if lay.slots > lay.experts * lay.main:
        outputs = jnp.concatenate([outputs, extra_rows[...].astype(BF16)], axis=0)
    onehot = slot_onehot(lay, ids_ref[...], scalars[0])
    picked = lax.dot_general(onehot, outputs, TN, preferred_element_type=F32)
    if has_gates:
        picked = picked * gates
    mixed = (tokens.astype(F32) + picked).astype(BF16)
    if has_first:
        out[0] = first[...]
        out[1] = mixed
    else:
        out[...] = mixed


def combine(lay, scalars, tokens, ids, gates, parts, fresh=None, first=None):
    args = [scalars, tokens, ids]
    if fresh is not None:
        args.append(fresh)
    if gates is not None:
        args.append(gates)
    if first is not None:
        args.append(first)
    args += list(parts)
    shape = (lay.tokens, lay.width)
    if first is not None:
        shape = (2,) + shape
    spare = max(8, lay.slots - lay.experts * lay.main)
    return call(
        functools.partial(
            combine_kernel, lay, gates is not None, fresh is not None, first is not None
        ),
        args,
        [jax.ShapeDtypeStruct(shape, BF16)],
        [stage_shape(lay), pltpu.VMEM((spare, lay.width), F32)],
        2 * lay.slots * lay.tokens * lay.width,
        smem_first=True,
    )[0]


def gradient_kernel(passes, *refs):
    wide = refs[: 2 * passes]
    narrow = refs[2 * passes : 5 * passes]
    grad_gate, grad_up, grad_down = refs[5 * passes :]

    def total(left, right):
        terms = [
            lax.dot_general(a[...], b[...], TN, preferred_element_type=F32)
            for a, b in zip(left, right)
        ]
        return functools.reduce(jnp.add, terms).astype(BF16)

    rows, cots = wide[:passes], wide[passes:]
    d_gate, d_up, hidden = narrow[:passes], narrow[passes : 2 * passes], narrow[2 * passes :]
    grad_gate[...] = total(rows, d_gate)
    grad_up[...] = total(rows, d_up)
    grad_down[...] = total(hidden, cots)


def gradients(kept, half):
    passes = len(kept)
    held, width = kept[0][0].shape
    tile = 2 * LANES if width % (2 * LANES) == 0 else width
    args = [k[i] for i in range(5) for k in kept]
    wide = pl.BlockSpec((held, tile), lambda i: (0, i))
    narrow = pl.BlockSpec((held, half), lambda i: (0, 0))
    tall = pl.BlockSpec((tile, half), lambda i: (i, 0))
    flat = pl.BlockSpec((half, tile), lambda i: (0, i))
    outs = [
        jax.ShapeDtypeStruct((width, half), BF16),
        jax.ShapeDtypeStruct((width, half), BF16),
        jax.ShapeDtypeStruct((half, width), BF16),
    ]
    return pl.pallas_call(
        functools.partial(gradient_kernel, passes),
        grid=(width // tile,),
        out_shape=outs,
        in_specs=[wide] * (2 * passes) + [narrow] * (3 * passes),
        out_specs=[tall, tall, flat],
        compiler_params=pltpu.CompilerParams(vmem_limit_bytes=VMEM_LIMIT),
        cost_estimate=cost(2 * 3 * passes * held * width * half, args + outs),
    )(*args)


def mirrored(value):
    count = lax.axis_size("section")
    return lax.ppermute(value, "section", [(i, count - 1 - i) for i in range(count)])


def passed_along(value, by):
    count = lax.axis_size("section")
    pairs = [(i, i + by) for i in range(count) if 0 <= i + by < count]
    return lax.ppermute(value, "section", pairs)


def per_device(
    left_in,
    left_new,
    left_saved,
    left_cot,
    right_in,
    right_saved,
    right_cot,
    right_cot_new,
    expert_ids,
    gate_values,
    w_gate,
    w_up,
    w_down,
):
    peers = lax.axis_size("expert")
    tokens, width = left_in.shape[1:]
    assert expert_ids.shape[-1] == 1
    lay = Layout(peers, tokens, width)
    weights = (w_gate[0, 0], w_up[0, 0], w_down[0, 0])
    half = w_gate.shape[-1]
    section = lax.axis_index("section")
    own_expert = lax.axis_index("expert") // 2
    is_first = (section == 0).astype(jnp.int32)
    is_last = (section == lax.axis_size("section") - 1).astype(jnp.int32)
    left_scalars = jnp.stack([own_expert, is_first]).astype(jnp.int32)
    right_scalars = jnp.stack([own_expert, is_last]).astype(jnp.int32)

    def ids(slot, side):
        return expert_ids[slot, side, 0]

    def gates(slot, side):
        return gate_values[slot, side, 0]

    saved_zero = mirrored(right_saved[0, 0])
    cot_zero = mirrored(right_cot[0])

    sent = route(lay, left_scalars, [(left_in[0], ids(0, 0), None, None)])
    rows_f0 = dispatch(lay, sent)
    sent = route(
        lay,
        left_scalars,
        [
            (left_saved[0], ids(1, 1), None, None),
            (left_cot[0], ids(1, 1), gates(1, 1), None),
        ],
    )
    rows_b1 = dispatch(lay, sent)
    parts_f0 = exchange(lay, forward(lay, rows_f0, 0, weights))
    left_zero = combine(lay, left_scalars, left_in[0], ids(0, 0), gates(0, 0), parts_f0)
    arriving = passed_along(left_zero, 1)

    right_first = mirrored(right_in[0])
    saved_two = mirrored(right_saved[1, 0])

    sent = route(
        lay,
        right_scalars,
        [(saved_zero, ids(0, 1), None, None), (cot_zero, ids(0, 1), gates(0, 1), None)],
    )
    rows_b0 = dispatch(lay, sent)
    parts, kept_b1 = backward(lay, rows_b1, 0, rows_b1, 1, weights)
    parts_b1 = exchange(lay, parts)
    back_one = combine(lay, right_scalars, left_cot[0], ids(1, 1), None, parts_b1)
    parts, kept_b0 = backward(lay, rows_b0, 0, rows_b0, 1, weights)
    parts_b0 = exchange(lay, parts)
    back_zero = combine(lay, right_scalars, cot_zero, ids(0, 1), None, parts_b0)
    returning = passed_along(back_zero, -1)

    sent = route(
        lay,
        right_scalars,
        [(right_first, ids(1, 0), None, None), (saved_two, ids(2, 1), None, None)],
    )
    rows_f1 = dispatch(lay, sent)
    sent = route(lay, left_scalars, [(arriving, ids(2, 0), None, left_new)])
    rows_f2 = dispatch(lay, sent)
    parts_f2 = exchange(lay, forward(lay, rows_f2, 0, weights))
    left_out = combine(
        lay, left_scalars, arriving, ids(2, 0), gates(2, 0), parts_f2, left_new, left_zero
    )
    parts_f1 = exchange(lay, forward(lay, rows_f1, 0, weights))
    right_out = combine(lay, right_scalars, right_first, ids(1, 0), gates(1, 0), parts_f1)

    sent = route(lay, right_scalars, [(returning, ids(2, 1), gates(2, 1), right_cot_new)])
    cots_b2 = dispatch(lay, sent)
    parts, kept_b2 = backward(lay, rows_f1, 1, cots_b2, 0, weights)
    parts_b2 = exchange(lay, parts)
    grad_gate, grad_up, grad_down = gradients((kept_b0, kept_b1, kept_b2), half)
    right_back = combine(
        lay, right_scalars, returning, ids(2, 1), None, parts_b2, right_cot_new, back_zero
    )
    return (
        left_out[:, None],
        right_out[None],
        back_one[None],
        right_back[:, None],
        grad_gate[None, None],
        grad_up[None, None],
        grad_down[None, None],
    )


def solution(mesh):
    in_specs = (
        P("section", "expert", None),
        P("expert", None),
        P("section", "expert", None),
        P("section", "expert", None),
        P("section", "expert", None),
        P(None, "section", "expert", None),
        P("section", "expert", None),
        P("expert", None),
        P(None, None, "section", "expert", None),
        P(None, None, "section", "expert", None),
        P("section", "expert", None, None),
        P("section", "expert", None, None),
        P("section", "expert", None, None),
    )
    out_specs = (
        P(None, "section", "expert", None),
        P("section", "expert", None),
        P("section", "expert", None),
        P(None, "section", "expert", None),
        P("section", "expert", None, None),
        P("section", "expert", None, None),
        P("section", "expert", None, None),
    )
    return jax.shard_map(
        per_device, mesh=mesh, in_specs=in_specs, out_specs=out_specs, check_vma=False
    )
```

```python
import functools

import jax
import jax.numpy as jnp
from jax import lax
from jax.experimental import pallas as pl
from jax.experimental.pallas import tpu as pltpu
from jax.sharding import PartitionSpec as P

LANES = 128
F32 = jnp.float32
BF16 = jnp.bfloat16
MIB = 1024 * 1024


class Layout:
    def __init__(self, peers, tokens, width):
        self.peers = peers
        self.experts = peers // 2
        self.tokens = tokens
        self.width = width
        self.cap = min(tokens, 2 * ((tokens // self.experts + 1) // 2) + 2)
        self.main = self.cap // 8 * 8
        self.extra = self.cap - self.main
        self.slabs = width // LANES
        self.per_group = self.main // self.extra if self.extra else 1
        self.groups = -(-self.slabs // self.per_group) if self.extra else 0
        self.packed = width + self.groups * LANES
        self.slots = -(-(self.experts * self.cap) // 16) * 16
        self.rows = peers * self.cap
        self.rows_held = -(-self.rows // 16) * 16


def slab_place(lay, slab):
    group, at = divmod(slab, lay.per_group)
    return at * lay.extra, lay.width + group * LANES


def pack_extra(lay, rows, start, out_ref, lead, stage):
    if not lay.extra:
        return
    if lay.slabs % lay.per_group:
        stage[...] = jnp.zeros_like(stage)
    part = rows[start : start + lay.extra, :]
    for slab in range(lay.slabs):
        row, col = slab_place(lay, slab)
        stage[row : row + lay.extra, col - lay.width : col - lay.width + LANES] = part[
            :, slab * LANES : (slab + 1) * LANES
        ]
    out_ref[lead, :, lay.width :] = stage[...].astype(BF16)


def unpack_extra(lay, packed, stage, into, row_at):
    stage[...] = packed
    for slab in range(lay.slabs):
        row, col = slab_place(lay, slab)
        into[row_at : row_at + lay.extra, slab * LANES : (slab + 1) * LANES] = stage[
            row : row + lay.extra, col - lay.width : col - lay.width + LANES
        ]


def stacked_main(lay, blocks):
    if lay.main % 16:
        return jnp.concatenate([b.astype(F32) for b in blocks], axis=0).astype(BF16)
    return jnp.concatenate(blocks, axis=0)


def as_column(row):
    square = (row.shape[1], row.shape[1])
    down = lax.broadcasted_iota(jnp.int32, square, 0)
    across = lax.broadcasted_iota(jnp.int32, square, 1)
    return jnp.sum(jnp.where(down == across, row, jnp.zeros_like(row)), axis=1, keepdims=True)


def slot_onehot(lay, ids_row):
    tokens = lay.tokens
    own_expert = lax.axis_index("expert") // 2
    down = lax.broadcasted_iota(jnp.int32, (tokens, tokens), 0)
    across = lax.broadcasted_iota(jnp.int32, (tokens, tokens), 1)
    earlier = jnp.logical_and(as_column(ids_row) == ids_row, down < across)
    rank = jnp.sum(earlier.astype(jnp.int32), axis=0, keepdims=True)
    near = ids_row ^ own_expert
    slot = jnp.where(
        rank < lay.main,
        near * lay.main + rank,
        lay.experts * lay.main + near * lay.extra + rank - lay.main,
    )
    place = lax.broadcasted_iota(jnp.int32, (lay.slots, tokens), 0)
    return (place == slot).astype(F32).astype(BF16)


def stage_shape(lay):
    return pltpu.VMEM((lay.main, max(1, lay.groups) * LANES), F32)


def at_edge(edge):
    last = lax.axis_size("section") - 1
    return lax.axis_index("section") == (0 if edge == "first" else last)


def route_kernel(lay, plan, ids, gates, *refs):
    at = 0
    items = []
    for which, lead, scaled, edge in plan:
        tokens = refs[at][...] if lead is None else refs[at][lead]
        at += 1
        if edge is not None:
            tokens = jnp.where(at_edge(edge), refs[at][...], tokens)
            at += 1
        items.append((which, scaled, tokens))
    outs = refs[len(refs) - 1 - lay.experts : len(refs) - 1]
    stage = refs[len(refs) - 1]
    onehots = {}
    for lead, (which, scaled, tokens) in enumerate(items):
        if which not in onehots:
            onehots[which] = slot_onehot(lay, ids[which])
        if scaled:
            tokens = (as_column(gates[which]) * tokens.astype(F32)).astype(BF16)
        rows = jnp.dot(onehots[which], tokens, preferred_element_type=F32)
        for j, out in enumerate(outs):
            out[lead, :, : lay.width] = rows[j * lay.main : (j + 1) * lay.main].astype(BF16)
            pack_extra(lay, rows, lay.experts * lay.main + j * lay.extra, out, lead, stage)


VMEM_SPEC = pl.BlockSpec(memory_space=pltpu.VMEM)
ANY_SPEC = pl.BlockSpec(memory_space=pl.ANY)


def cost(flops, arrays):
    moved = sum(a.size * a.dtype.itemsize for a in arrays)
    return pl.CostEstimate(flops=int(flops), bytes_accessed=int(moved), transcendentals=0)


def call(kernel, args, outs, scratch, flops, limit, after=()):
    specs = [VMEM_SPEC] * len(args) + [ANY_SPEC] * len(after)

    def body(*refs):
        kernel(*refs[: len(args)], *refs[len(args) + len(after) :])

    return pl.pallas_call(
        body,
        out_shape=outs,
        in_specs=specs,
        out_specs=[VMEM_SPEC] * len(outs),
        scratch_shapes=scratch,
        compiler_params=pltpu.CompilerParams(vmem_limit_bytes=limit * MIB),
        cost_estimate=cost(flops, list(args) + list(outs)),
    )(*args, *after)


def route(lay, tables, items, after=()):
    args = list(tables)
    plan = []
    for tokens, lead, which, scaled, edge, fresh in items:
        args.append(tokens)
        if fresh is not None:
            args.append(fresh)
        plan.append((which, lead, scaled, edge))
    out = jax.ShapeDtypeStruct((len(items), lay.main, lay.packed), BF16)
    return call(
        functools.partial(route_kernel, lay, tuple(plan)),
        args,
        [out] * lay.experts,
        [stage_shape(lay)],
        2 * lay.slots * lay.tokens * lay.width * len(items),
        8,
        after,
    )


def stack_kernel(picks, *refs):
    count = len(picks)
    out, sems = refs[count], refs[count + 1]
    copies = []
    for at, pick in enumerate(picks):
        source = refs[at]
        for i in pick:
            source = source.at[i]
        copies.append(pltpu.make_async_copy(source, out.at[at], sems.at[at]))
    for copy in copies:
        copy.start()
    for copy in copies:
        copy.wait()


def stacked(lay, arrays, picks, after=()):
    count = len(arrays)

    def body(*refs):
        stack_kernel(picks, *refs[:count], *refs[count + len(after) :])

    out = jax.ShapeDtypeStruct((count, lay.tokens, lay.width), BF16)
    return pl.pallas_call(
        body,
        out_shape=out,
        in_specs=[ANY_SPEC] * (count + len(after)),
        out_specs=VMEM_SPEC,
        scratch_shapes=[pltpu.SemaphoreType.DMA((count,))],
        compiler_params=pltpu.CompilerParams(vmem_limit_bytes=2 * MIB),
        cost_estimate=cost(0, [out, out]),
    )(*arrays, *after)


def exchange(lay, by_distance):
    got = [by_distance[0]]
    for d in range(1, lay.peers):
        pairs = [(i, i ^ d) for i in range(lay.peers)]
        got.append(lax.ppermute(by_distance[d], "expert", pairs))
    return got


def dispatch(lay, payloads):
    return exchange(lay, [payloads[d // 2] for d in range(lay.peers)])


def load_rows(lay, refs, lead, stage, extra_rows):
    main = stacked_main(lay, [r[lead, :, : lay.width] for r in refs])
    if not lay.extra:
        return main
    extra_rows[...] = jnp.zeros_like(extra_rows)
    for d, ref in enumerate(refs):
        unpack_extra(lay, ref[lead, :, lay.width :].astype(F32), stage, extra_rows, d * lay.extra)
    return jnp.concatenate([main, extra_rows[...].astype(BF16)], axis=0)


def store_parts(lay, rows, refs, stage):
    for d, ref in enumerate(refs):
        ref[0, :, : lay.width] = rows[d * lay.main : (d + 1) * lay.main].astype(BF16)
        pack_extra(lay, rows, lay.peers * lay.main + d * lay.extra, ref, 0, stage)


def extra_shape(lay):
    return pltpu.VMEM((lay.rows_held - lay.peers * lay.main, lay.width), F32)


NT = (((1,), (1,)), ((), ()))
TN = (((0,), (0,)), ((), ()))


def forward_kernel(lay, lead, *refs):
    blocks = refs[: lay.peers]
    w_gate, w_up, w_down = refs[lay.peers : lay.peers + 3]
    outs = refs[lay.peers + 3 : 2 * lay.peers + 3]
    stage, extra_rows = refs[2 * lay.peers + 3 :]
    rows = load_rows(lay, blocks, lead, stage, extra_rows)
    gate = jnp.dot(rows, w_gate[...], preferred_element_type=F32)
    up = jnp.dot(rows, w_up[...], preferred_element_type=F32)
    hidden = (gate * jax.nn.sigmoid(gate) * up).astype(BF16)
    part = jnp.dot(hidden, w_down[...], preferred_element_type=F32)
    store_parts(lay, part, outs, stage)


def forward(lay, blocks, lead, weights, after=()):
    out = jax.ShapeDtypeStruct((1, lay.main, lay.packed), BF16)
    return call(
        functools.partial(forward_kernel, lay, lead),
        list(blocks) + list(weights),
        [out] * lay.peers,
        [stage_shape(lay), extra_shape(lay)],
        2 * 3 * lay.rows * lay.width * weights[0].shape[1],
        14,
        after,
    )


def backward_kernel(lay, row_lead, cot_lead, *refs):
    n = lay.peers
    row_blocks, cot_blocks = refs[:n], refs[n : 2 * n]
    w_gate, w_up, w_down = refs[2 * n : 2 * n + 3]
    outs = refs[2 * n + 3 : 3 * n + 3]
    rows_out, cot_out, d_both_out, hidden_out = refs[3 * n + 3 : 3 * n + 7]
    stage, extra_rows = refs[3 * n + 7 :]
    rows = load_rows(lay, row_blocks, row_lead, stage, extra_rows)
    rows_out[...] = rows
    gate = jnp.dot(rows, w_gate[...], preferred_element_type=F32)
    up = jnp.dot(rows, w_up[...], preferred_element_type=F32)
    row_cot = load_rows(lay, cot_blocks, cot_lead, stage, extra_rows)
    cot_out[...] = row_cot
    d_hidden = lax.dot_general(row_cot, w_down[...], NT, preferred_element_type=F32)
    logistic = jax.nn.sigmoid(gate)
    swish = gate * logistic
    hidden_out[...] = (swish * up).astype(BF16)
    d_gate = (d_hidden * up * logistic * (1.0 + gate * (1.0 - logistic))).astype(BF16)
    d_up = (d_hidden * swish).astype(BF16)
    half = d_gate.shape[1]
    d_both_out[:, :half] = d_gate
    d_both_out[:, half:] = d_up
    back = lax.dot_general(d_gate, w_gate[...], NT, preferred_element_type=F32)
    back = back + lax.dot_general(d_up, w_up[...], NT, preferred_element_type=F32)
    store_parts(lay, back, outs, stage)


def backward(lay, rows, row_lead, cots, cot_lead, weights, after=()):
    half = weights[0].shape[1]
    out = jax.ShapeDtypeStruct((1, lay.main, lay.packed), BF16)
    wide = jax.ShapeDtypeStruct((lay.rows_held, lay.width), BF16)
    both = jax.ShapeDtypeStruct((lay.rows_held, 2 * half), BF16)
    narrow = jax.ShapeDtypeStruct((lay.rows_held, half), BF16)
    got = call(
        functools.partial(backward_kernel, lay, row_lead, cot_lead),
        list(rows) + list(cots) + list(weights),
        [out] * lay.peers + [wide, wide, both, narrow],
        [stage_shape(lay), extra_shape(lay)],
        2 * 5 * lay.rows * lay.width * half,
        18,
        after,
    )
    return got[: lay.peers], got[lay.peers :]


def combine_kernel(lay, which, lead, scaled, edge, has_first, ids, gates, tokens_ref, *refs):
    at = 0
    tokens = tokens_ref[...] if lead is None else tokens_ref[lead]
    if edge is not None:
        tokens = jnp.where(at_edge(edge), refs[at][...], tokens)
        at += 1
    if has_first:
        first = refs[at]
        at += 1
    parts = refs[at : at + lay.peers]
    out, stage, extra_rows = refs[at + lay.peers :]
    mains = []
    if lay.extra:
        extra_rows[...] = jnp.zeros_like(extra_rows)
    for j in range(lay.experts):
        total = parts[2 * j][0].astype(F32) + parts[2 * j + 1][0].astype(F32)
        mains.append(total[:, : lay.width].astype(BF16))
        if lay.extra:
            unpack_extra(lay, total[:, lay.width :], stage, extra_rows, j * lay.extra)
    outputs = stacked_main(lay, mains)
    if lay.slots > lay.experts * lay.main:
        outputs = jnp.concatenate([outputs, extra_rows[...].astype(BF16)], axis=0)
    onehot = slot_onehot(lay, ids[which])
    picked = lax.dot_general(onehot, outputs, TN, preferred_element_type=F32)
    if scaled:
        picked = picked * as_column(gates[which])
    mixed = (tokens.astype(F32) + picked).astype(BF16)
    if has_first:
        out[0] = first[...]
        out[1] = mixed
    else:
        out[...] = mixed


def combine(
    lay, tables, which, scaled, tokens, parts, lead=None, edge=None, fresh=None, first=None, after=()
):
    args = list(tables) + [tokens]
    if fresh is not None:
        args.append(fresh)
    if first is not None:
        args.append(first)
    args += list(parts)
    shape = (lay.tokens, lay.width)
    if first is not None:
        shape = (2,) + shape
    spare = max(8, lay.slots - lay.experts * lay.main)
    return call(
        functools.partial(combine_kernel, lay, which, lead, scaled, edge, first is not None),
        args,
        [jax.ShapeDtypeStruct(shape, BF16)],
        [stage_shape(lay), pltpu.VMEM((spare, lay.width), F32)],
        2 * lay.slots * lay.tokens * lay.width,
        8,
        after,
    )[0]


def gradient_kernel(passes, *refs):
    rows, cots, both, hidden = (
        jnp.concatenate([r[...] for r in refs[i * passes : (i + 1) * passes]], axis=0)
        for i in range(4)
    )
    grad_gate, grad_up, grad_down = refs[4 * passes :]
    half = hidden.shape[1]
    total = lax.dot_general(rows, both, TN, preferred_element_type=F32)
    grad_gate[...] = total[:, :half].astype(BF16)
    grad_up[...] = total[:, half:].astype(BF16)
    grad_down[...] = lax.dot_general(hidden, cots, TN, preferred_element_type=F32).astype(BF16)


def gradients(kept, half):
    passes = len(kept)
    held, width = kept[0][0].shape
    tile = 2 * LANES if width % (2 * LANES) == 0 else width
    args = [k[i] for i in range(4) for k in kept]
    wide = pl.BlockSpec((held, tile), lambda i: (0, i))
    both = pl.BlockSpec((held, 2 * half), lambda i: (0, 0))
    narrow = pl.BlockSpec((held, half), lambda i: (0, 0))
    tall = pl.BlockSpec((tile, half), lambda i: (i, 0))
    flat = pl.BlockSpec((half, tile), lambda i: (0, i))
    outs = [
        jax.ShapeDtypeStruct((width, half), BF16),
        jax.ShapeDtypeStruct((width, half), BF16),
        jax.ShapeDtypeStruct((half, width), BF16),
    ]
    return pl.pallas_call(
        functools.partial(gradient_kernel, passes),
        grid=(width // tile,),
        out_shape=outs,
        in_specs=[wide] * (2 * passes) + [both] * passes + [narrow] * passes,
        out_specs=[tall, tall, flat],
        compiler_params=pltpu.CompilerParams(vmem_limit_bytes=16 * MIB),
        cost_estimate=cost(2 * 3 * passes * held * width * half, args + outs),
    )(*args)


def mirrored(value):
    count = lax.axis_size("section")
    return lax.ppermute(value, "section", [(i, count - 1 - i) for i in range(count)])


def passed_along(value, by):
    count = lax.axis_size("section")
    pairs = [(i, i + by) for i in range(count) if 0 <= i + by < count]
    return lax.ppermute(value, "section", pairs)


def per_device(
    left_in,
    left_new,
    left_saved,
    left_cot,
    right_in,
    right_saved,
    right_cot,
    right_cot_new,
    expert_ids,
    gate_values,
    w_gate,
    w_up,
    w_down,
):
    peers = lax.axis_size("expert")
    tokens, width = left_in.shape[1:]
    assert expert_ids.shape[-1] == 1
    lay = Layout(peers, tokens, width)
    weights = (w_gate[0, 0], w_up[0, 0], w_down[0, 0])
    half = w_gate.shape[-1]
    slots = expert_ids.shape[0]
    tables = (
        expert_ids.reshape(2 * slots, 1, tokens),
        gate_values.reshape(2 * slots, 1, tokens),
    )
    f0, b0, f1, b1, f2, b2 = range(2 * slots)

    mirror_zero = mirrored(stacked(lay, (right_saved, right_cot), ((0, 0), (0,))))

    rows_f0 = dispatch(lay, route(lay, tables, [(left_in[0], None, f0, False, None, None)]))
    sent = route(
        lay,
        tables,
        [
            (left_saved[0], None, b1, False, None, None),
            (left_cot[0], None, b1, True, None, None),
        ],
    )
    rows_b1 = dispatch(lay, sent)
    parts_f0 = exchange(lay, forward(lay, rows_f0, 0, weights))
    parts, kept_b1 = backward(lay, rows_b1, 0, rows_b1, 1, weights)
    parts_b1 = exchange(lay, parts)
    left_zero = combine(lay, tables, f0, True, left_in[0], parts_f0)
    arriving = passed_along(left_zero, 1)

    sent = route(
        lay,
        tables,
        [(mirror_zero, 0, b0, False, None, None), (mirror_zero, 1, b0, True, None, None)],
        after=(left_zero,),
    )
    rows_b0 = dispatch(lay, sent)
    mirror_one = mirrored(
        stacked(lay, (right_in, right_saved), ((0,), (1, 0)), after=(sent[0],))
    )
    back_one = combine(lay, tables, b1, False, left_cot[0], parts_b1, after=(sent[0],))

    sent = route(
        lay, tables, [(arriving, None, f2, False, "first", left_new)], after=(rows_b0[1],)
    )
    rows_f2 = dispatch(lay, sent)
    parts, kept_b0 = backward(lay, rows_b0, 0, rows_b0, 1, weights)
    parts_b0 = exchange(lay, parts)
    parts_f2 = exchange(lay, forward(lay, rows_f2, 0, weights, after=(parts[0],)))
    back_zero = combine(lay, tables, b0, False, mirror_zero, parts_b0, lead=1)
    returning = passed_along(back_zero, -1)

    sent = route(
        lay,
        tables,
        [(mirror_one, 0, f1, False, None, None), (mirror_one, 1, b2, False, None, None)],
        after=(back_zero,),
    )
    rows_f1 = dispatch(lay, sent)
    left_out = combine(
        lay,
        tables,
        f2,
        True,
        arriving,
        parts_f2,
        edge="first",
        fresh=left_new,
        first=left_zero,
        after=(sent[0],),
    )

    sent = route(lay, tables, [(returning, None, b2, True, "last", right_cot_new)])
    cots_b2 = dispatch(lay, sent)
    parts_f1 = exchange(lay, forward(lay, rows_f1, 0, weights, after=(sent[0],)))
    parts, kept_b2 = backward(lay, rows_f1, 1, cots_b2, 0, weights)
    parts_b2 = exchange(lay, parts)
    right_out = combine(lay, tables, f1, True, mirror_one, parts_f1, lead=0, after=(parts[0],))
    grad_gate, grad_up, grad_down = gradients((kept_b0, kept_b1, kept_b2), half)
    right_back = combine(
        lay,
        tables,
        b2,
        False,
        returning,
        parts_b2,
        edge="last",
        fresh=right_cot_new,
        first=back_zero,
    )
    return (
        left_out[:, None],
        right_out[None],
        back_one[None],
        right_back[:, None],
        grad_gate[None, None],
        grad_up[None, None],
        grad_down[None, None],
    )


def solution(mesh):
    in_specs = (
        P("section", "expert", None),
        P("expert", None),
        P("section", "expert", None),
        P("section", "expert", None),
        P("section", "expert", None),
        P(None, "section", "expert", None),
        P("section", "expert", None),
        P("expert", None),
        P(None, None, "section", "expert", None),
        P(None, None, "section", "expert", None),
        P("section", "expert", None, None),
        P("section", "expert", None, None),
        P("section", "expert", None, None),
    )
    out_specs = (
        P(None, "section", "expert", None),
        P("section", "expert", None),
        P("section", "expert", None),
        P(None, "section", "expert", None),
        P("section", "expert", None, None),
        P("section", "expert", None, None),
        P("section", "expert", None, None),
    )
    return jax.shard_map(
        per_device, mesh=mesh, in_specs=in_specs, out_specs=out_specs, check_vma=False
    )
```

```python
import functools

import jax
import jax.numpy as jnp
from jax import lax
from jax.experimental import pallas as pl
from jax.experimental.pallas import tpu as pltpu
from jax.sharding import PartitionSpec as P

LANES = 128
F32 = jnp.float32
BF16 = jnp.bfloat16
MIB = 1024 * 1024


class Layout:
    def __init__(self, peers, tokens, width):
        self.peers = peers
        self.experts = peers // 2
        self.tokens = tokens
        self.width = width
        self.cap = min(tokens, 2 * ((tokens // self.experts + 1) // 2) + 2)
        self.main = self.cap // 8 * 8
        self.extra = self.cap - self.main
        self.slabs = width // LANES
        self.per_group = self.main // self.extra if self.extra else 1
        self.groups = -(-self.slabs // self.per_group) if self.extra else 0
        self.packed = width + self.groups * LANES
        self.slots = -(-(self.experts * self.cap) // 16) * 16
        self.rows = peers * self.cap
        self.rows_held = -(-self.rows // 16) * 16


def slab_place(lay, slab):
    group, at = divmod(slab, lay.per_group)
    return at * lay.extra, lay.width + group * LANES


def pack_extra(lay, rows, start, out_ref, lead, stage):
    if not lay.extra:
        return
    if lay.slabs % lay.per_group:
        stage[...] = jnp.zeros_like(stage)
    part = rows[start : start + lay.extra, :]
    for slab in range(lay.slabs):
        row, col = slab_place(lay, slab)
        stage[row : row + lay.extra, col - lay.width : col - lay.width + LANES] = part[
            :, slab * LANES : (slab + 1) * LANES
        ]
    out_ref[lead, :, lay.width :] = stage[...].astype(BF16)


def unpack_extra(lay, packed, stage, into, row_at):
    stage[...] = packed
    for slab in range(lay.slabs):
        row, col = slab_place(lay, slab)
        into[row_at : row_at + lay.extra, slab * LANES : (slab + 1) * LANES] = stage[
            row : row + lay.extra, col - lay.width : col - lay.width + LANES
        ]


def stacked_main(lay, blocks):
    if lay.main % 16:
        return jnp.concatenate([b.astype(F32) for b in blocks], axis=0).astype(BF16)
    return jnp.concatenate(blocks, axis=0)


def as_column(row):
    square = (row.shape[1], row.shape[1])
    down = lax.broadcasted_iota(jnp.int32, square, 0)
    across = lax.broadcasted_iota(jnp.int32, square, 1)
    return jnp.sum(jnp.where(down == across, row, jnp.zeros_like(row)), axis=1, keepdims=True)


def slot_onehot(lay, ids_row):
    tokens = lay.tokens
    own_expert = lax.axis_index("expert") // 2
    down = lax.broadcasted_iota(jnp.int32, (tokens, tokens), 0)
    across = lax.broadcasted_iota(jnp.int32, (tokens, tokens), 1)
    earlier = jnp.logical_and(as_column(ids_row) == ids_row, down < across)
    rank = jnp.sum(earlier.astype(jnp.int32), axis=0, keepdims=True)
    near = ids_row ^ own_expert
    slot = jnp.where(
        rank < lay.main,
        near * lay.main + rank,
        lay.experts * lay.main + near * lay.extra + rank - lay.main,
    )
    place = lax.broadcasted_iota(jnp.int32, (lay.slots, tokens), 0)
    return (place == slot).astype(F32).astype(BF16)


def stage_shape(lay):
    return pltpu.VMEM((lay.main, max(1, lay.groups) * LANES), F32)


def at_edge(edge):
    last = lax.axis_size("section") - 1
    return lax.axis_index("section") == (0 if edge == "first" else last)


def route_kernel(lay, plan, groups, loads, *refs):
    inputs = sum(1 if edge is None else 2 for *_, edge in plan)
    ids, gates = refs[inputs : inputs + 2]
    outs = refs[inputs + 2 : inputs + 2 + len(groups) * lay.experts]
    scratch = refs[inputs + 2 + len(outs) :]
    stage = scratch[0]
    copies = []
    for i in range(loads):
        copies.append(pltpu.make_async_copy(refs[i], scratch[1].at[i], scratch[2].at[i]))
        copies[-1].start()
    onehots = {which: slot_onehot(lay, ids[which]) for which, *_ in plan}

    def read(at, lead):
        if loads:
            copies[at].wait()
            return scratch[1][at]
        return refs[at][...] if lead is None else refs[at][lead]

    at = 0
    places = [(g, lead) for g, size in enumerate(groups) for lead in range(size)]
    for (group, place), (which, lead, scaled, edge) in zip(places, plan):
        tokens = read(at, lead)
        at += 1
        if edge is not None:
            tokens = jnp.where(at_edge(edge), read(at, None), tokens)
            at += 1
        if scaled:
            tokens = (as_column(gates[which]) * tokens.astype(F32)).astype(BF16)
        rows = jnp.dot(onehots[which], tokens, preferred_element_type=F32)
        for j in range(lay.experts):
            out = outs[group * lay.experts + j]
            out[place, :, : lay.width] = rows[j * lay.main : (j + 1) * lay.main].astype(BF16)
            pack_extra(lay, rows, lay.experts * lay.main + j * lay.extra, out, place, stage)


VMEM_SPEC = pl.BlockSpec(memory_space=pltpu.VMEM)
ANY_SPEC = pl.BlockSpec(memory_space=pl.ANY)
HBM_SPEC = pl.BlockSpec(memory_space=pltpu.HBM)


def cost(flops, arrays):
    moved = sum(a.size * a.dtype.itemsize for a in arrays)
    return pl.CostEstimate(flops=int(flops), bytes_accessed=int(moved), transcendentals=0)


class Chain:
    def __init__(self):
        self.last = ()


def call(chain, kernel, args, outs, scratch, flops, limit, in_hbm=0):
    after = chain.last
    specs = [HBM_SPEC] * in_hbm + [VMEM_SPEC] * (len(args) - in_hbm) + [ANY_SPEC] * len(after)

    def body(*refs):
        kernel(*refs[: len(args)], *refs[len(args) + len(after) :])

    got = pl.pallas_call(
        body,
        out_shape=outs,
        in_specs=specs,
        out_specs=[VMEM_SPEC] * len(outs),
        scratch_shapes=scratch,
        compiler_params=pltpu.CompilerParams(vmem_limit_bytes=limit * MIB),
        cost_estimate=cost(flops, list(args) + list(outs)),
    )(*args, *after)
    chain.last = (got[0],)
    return got


def route(lay, chain, tables, items, groups, in_hbm=False, limit=10):
    args = []
    plan = []
    for tokens, lead, which, scaled, edge, fresh in items:
        args.append(tokens)
        if fresh is not None:
            args.append(fresh)
        plan.append((which, lead, scaled, edge))
    loads = len(args) if in_hbm else 0
    outs = [
        jax.ShapeDtypeStruct((size, lay.main, lay.packed), BF16)
        for size in groups
        for _ in range(lay.experts)
    ]
    scratch = [stage_shape(lay)]
    if loads:
        scratch += [
            pltpu.VMEM((loads, lay.tokens, lay.width), BF16),
            pltpu.SemaphoreType.DMA((loads,)),
        ]
    got = call(
        chain,
        functools.partial(route_kernel, lay, tuple(plan), tuple(groups), loads),
        args + list(tables),
        outs,
        scratch,
        2 * lay.slots * lay.tokens * lay.width * len(items),
        limit,
        loads,
    )
    return [got[g * lay.experts : (g + 1) * lay.experts] for g in range(len(groups))]


def stack_kernel(picks, *refs):
    count = len(picks)
    out, sems = refs[count], refs[count + 1]
    copies = []
    for at, pick in enumerate(picks):
        source = refs[at]
        for i in pick:
            source = source.at[i]
        copies.append(pltpu.make_async_copy(source, out.at[at], sems.at[at]))
    for copy in copies:
        copy.start()
    for copy in copies:
        copy.wait()


def stacked(lay, chain, arrays, picks, limit=4):
    count = len(arrays)
    out = jax.ShapeDtypeStruct((count, lay.tokens, lay.width), BF16)
    scratch = [pltpu.SemaphoreType.DMA((count,))]
    kernel = functools.partial(stack_kernel, tuple(picks))
    return call(chain, kernel, arrays, [out], scratch, 0, limit, count)[0]


def swapped(lay, value, bits):
    return lax.ppermute(value, "expert", [(i, i ^ bits) for i in range(lay.peers)])


def dispatch(lay, payloads, direct=False):
    got = []
    for j, payload in enumerate(payloads):
        here = payload if j == 0 else swapped(lay, payload, 2 * j)
        over = swapped(lay, payload, 2 * j + 1) if direct else swapped(lay, here, 1)
        got += [here, over]
    return got


def add_kernel(left, right, out):
    out[...] = (left[...].astype(F32) + right[...].astype(F32)).astype(BF16)


def handed_over(lay, parts, direct=False):
    if direct:
        return [parts[0]] + [swapped(lay, parts[d], d) for d in range(1, lay.peers)]
    return [swapped(lay, parts[2 * j + 1], 1) for j in range(lay.experts)]


def summed(lay, chain, parts, others):
    if len(others) == lay.peers:
        return others
    totals = []
    for j in range(1, lay.experts):
        other = others[j]
        out = jax.ShapeDtypeStruct(other.shape, BF16)
        total = call(chain, add_kernel, [parts[2 * j], other], [out], [], 2 * other.size, 4)[0]
        totals.append(swapped(lay, total, 2 * j))
    return [parts[0], others[0]] + totals


def load_rows(lay, refs, lead, stage, extra_rows):
    main = stacked_main(lay, [r[lead, :, : lay.width] for r in refs])
    if not lay.extra:
        return main
    extra_rows[...] = jnp.zeros_like(extra_rows)
    for d, ref in enumerate(refs):
        unpack_extra(lay, ref[lead, :, lay.width :].astype(F32), stage, extra_rows, d * lay.extra)
    return jnp.concatenate([main, extra_rows[...].astype(BF16)], axis=0)


def store_parts(lay, rows, refs, lead, stage):
    for d, ref in enumerate(refs):
        ref[lead, :, : lay.width] = rows[d * lay.main : (d + 1) * lay.main].astype(BF16)
        pack_extra(lay, rows, lay.peers * lay.main + d * lay.extra, ref, lead, stage)


def extra_shape(lay):
    return pltpu.VMEM((lay.rows_held - lay.peers * lay.main, lay.width), F32)


NT = (((1,), (1,)), ((), ()))
TN = (((0,), (0,)), ((), ()))


def expert_kernel(lay, tasks, groups, *refs):
    n = lay.peers
    blocks = [refs[g * n : (g + 1) * n] for g in range(groups)]
    at = groups * n
    w_gate, w_up, w_down = refs[at : at + 3]
    outs = refs[at + 3 : at + 3 + n]
    kept = refs[at + 3 + n : len(refs) - 2]
    stage, extra_rows = refs[len(refs) - 2 :]
    for task, (kind, *sources) in enumerate(tasks):
        held = [load_rows(lay, blocks[g], lead, stage, extra_rows) for g, lead in sources]
        rows = held[0]
        gate = jnp.dot(rows, w_gate[...], preferred_element_type=F32)
        up = jnp.dot(rows, w_up[...], preferred_element_type=F32)
        logistic = jax.nn.sigmoid(gate)
        swish = gate * logistic
        hidden = (swish * up).astype(BF16)
        if kind == "forward":
            part = jnp.dot(hidden, w_down[...], preferred_element_type=F32)
            store_parts(lay, part, outs, task, stage)
            continue
        row_cot = held[1]
        d_hidden = lax.dot_general(row_cot, w_down[...], NT, preferred_element_type=F32)
        d_gate = (d_hidden * up * logistic * (1.0 + gate * (1.0 - logistic))).astype(BF16)
        d_up = (d_hidden * swish).astype(BF16)
        back = lax.dot_general(d_gate, w_gate[...], NT, preferred_element_type=F32)
        back = back + lax.dot_general(d_up, w_up[...], NT, preferred_element_type=F32)
        store_parts(lay, back, outs, task, stage)
        rows_out, cot_out, both_out, hidden_out = kept[:4]
        kept = kept[4:]
        half = d_gate.shape[1]
        rows_out[...] = rows
        cot_out[...] = row_cot
        both_out[:, :half] = d_gate
        both_out[:, half:] = d_up
        hidden_out[...] = hidden


def run_experts(lay, chain, tasks, groups, weights):
    half = weights[0].shape[1]
    out = jax.ShapeDtypeStruct((len(tasks), lay.main, lay.packed), BF16)
    wide = jax.ShapeDtypeStruct((lay.rows_held, lay.width), BF16)
    both = jax.ShapeDtypeStruct((lay.rows_held, 2 * half), BF16)
    narrow = jax.ShapeDtypeStruct((lay.rows_held, half), BF16)
    backs = sum(task[0] == "backward" for task in tasks)
    products = 3 * (len(tasks) - backs) + 5 * backs
    got = call(
        chain,
        functools.partial(expert_kernel, lay, tuple(tasks), len(groups)),
        [block for group in groups for block in group] + list(weights),
        [out] * lay.peers + [wide, wide, both, narrow] * backs,
        [stage_shape(lay), extra_shape(lay)],
        2 * products * lay.rows * lay.width * half,
        20,
    )
    kept = got[lay.peers :]
    return got[: lay.peers], [tuple(kept[4 * i : 4 * i + 4]) for i in range(backs)]


def mixed_tokens(lay, tokens, parts, task, ids_row, gates_row, stage, extra_rows):
    pairs = [[parts[0], parts[1]]]
    if len(parts) == lay.peers:
        pairs += [[parts[2 * j], parts[2 * j + 1]] for j in range(1, lay.experts)]
    else:
        pairs += [[part] for part in parts[2:]]
    mains = []
    if lay.extra:
        extra_rows[...] = jnp.zeros_like(extra_rows)
    for j in range(lay.experts):
        total = functools.reduce(jnp.add, [part[task].astype(F32) for part in pairs[j]])
        mains.append(total[:, : lay.width].astype(BF16))
        if lay.extra:
            unpack_extra(lay, total[:, lay.width :], stage, extra_rows, j * lay.extra)
    outputs = stacked_main(lay, mains)
    if lay.slots > lay.experts * lay.main:
        outputs = jnp.concatenate([outputs, extra_rows[...].astype(BF16)], axis=0)
    onehot = slot_onehot(lay, ids_row)
    picked = lax.dot_general(onehot, outputs, TN, preferred_element_type=F32)
    if gates_row is not None:
        picked = picked * as_column(gates_row)
    return (tokens.astype(F32) + picked).astype(BF16)


def combine_kernel(lay, which, lead, scaled, edge, has_first, task, ids, gates, tokens_ref, *refs):
    at = 0
    tokens = tokens_ref[...] if lead is None else tokens_ref[lead]
    if edge is not None:
        tokens = jnp.where(at_edge(edge), refs[at][...], tokens)
        at += 1
    if has_first:
        first = refs[at]
        at += 1
    parts = refs[at : len(refs) - 3]
    out, stage, extra_rows = refs[len(refs) - 3 :]
    gates_row = gates[which] if scaled else None
    mixed = mixed_tokens(lay, tokens, parts, task, ids[which], gates_row, stage, extra_rows)
    if has_first:
        out[0] = first[...]
        out[1] = mixed
    else:
        out[...] = mixed


def combine(
    lay,
    chain,
    tables,
    which,
    scaled,
    tokens,
    parts,
    task,
    lead=None,
    edge=None,
    fresh=None,
    first=None,
):
    args = list(tables) + [tokens]
    if fresh is not None:
        args.append(fresh)
    if first is not None:
        args.append(first)
    args += list(parts)
    shape = (lay.tokens, lay.width)
    if first is not None:
        shape = (2,) + shape
    spare = max(8, lay.slots - lay.experts * lay.main)
    return call(
        chain,
        functools.partial(
            combine_kernel, lay, which, lead, scaled, edge, first is not None, task
        ),
        args,
        [jax.ShapeDtypeStruct(shape, BF16)],
        [stage_shape(lay), pltpu.VMEM((spare, lay.width), F32)],
        2 * lay.slots * lay.tokens * lay.width,
        8,
    )[0]


def all_gradients_kernel(passes, *refs):
    rows, cots, both, hidden = (
        jnp.concatenate([r[...] for r in refs[i * passes : (i + 1) * passes]], axis=0)
        for i in range(4)
    )
    grad_gate, grad_up, grad_down = refs[4 * passes :]
    half = hidden.shape[1]

    total = lax.dot_general(rows, both, TN, preferred_element_type=F32)
    grad_gate[...] = total[:, :half].astype(BF16)
    grad_up[...] = total[:, half:].astype(BF16)
    grad_down[...] = lax.dot_general(hidden, cots, TN, preferred_element_type=F32).astype(BF16)


def all_gradients(chain, kept):
    after = chain.last
    passes = len(kept)
    held, width = kept[0][0].shape
    half = kept[0][3].shape[1]
    tile = 4 * LANES if width % (4 * LANES) == 0 else width
    args = [k[i] for i in range(4) for k in kept]
    wide = pl.BlockSpec((held, tile), lambda i: (0, i))
    both = pl.BlockSpec((held, 2 * half), lambda i: (0, 0))
    narrow = pl.BlockSpec((held, half), lambda i: (0, 0))
    tall = pl.BlockSpec((tile, half), lambda i: (i, 0))
    flat = pl.BlockSpec((half, tile), lambda i: (0, i))
    outs = [
        jax.ShapeDtypeStruct((width, half), BF16),
        jax.ShapeDtypeStruct((width, half), BF16),
        jax.ShapeDtypeStruct((half, width), BF16),
    ]

    def body(*refs):
        all_gradients_kernel(passes, *refs[: len(args)], *refs[len(args) + len(after) :])

    return pl.pallas_call(
        body,
        grid=(width // tile,),
        out_shape=outs,
        in_specs=[wide] * (2 * passes) + [both] * passes + [narrow] * passes
        + [ANY_SPEC] * len(after),
        out_specs=[tall, tall, flat],
        compiler_params=pltpu.CompilerParams(vmem_limit_bytes=20 * MIB),
        cost_estimate=cost(2 * 3 * passes * held * width * half, args + outs),
    )(*args, *after)


def opening_kernel(lay, plan, groups, picks, *refs):
    loads, stacks = len(plan), len(picks)
    tokens_in, ids_in, gates_in = refs[:loads], refs[loads], refs[loads + 1]
    stacked_in = refs[loads + 2 : loads + 2 + stacks]
    stack_out = refs[loads + 2 + stacks]
    outs = refs[loads + 3 + stacks : loads + 3 + stacks + len(groups) * lay.experts]
    stage, held, ids, gates, sems = refs[loads + 3 + stacks + len(outs) :]
    places = [(g, lead) for g, size in enumerate(groups) for lead in range(size)]
    sources = []
    for at, pick in enumerate(picks):
        source = stacked_in[at]
        for i in pick:
            source = source.at[i]
        sources.append(source)
    copies = [
        pltpu.make_async_copy(ids_in, ids, sems.at[0]),
        pltpu.make_async_copy(gates_in, gates, sems.at[1]),
    ]
    copies += [
        pltpu.make_async_copy(tokens_in[i], held.at[i], sems.at[2 + i]) for i in range(loads)
    ]
    copies += [
        pltpu.make_async_copy(source, stack_out.at[at], sems.at[2 + loads + at])
        for at, source in enumerate(sources)
    ]
    for copy in copies:
        copy.start()
    copies[0].wait()
    copies[1].wait()
    onehots = {which: slot_onehot(lay, ids[which]) for which, _ in plan}
    for at, ((group, place), (which, scaled)) in enumerate(zip(places, plan)):
        copies[2 + at].wait()
        tokens = held[at]
        if scaled:
            tokens = (as_column(gates[which]) * tokens.astype(F32)).astype(BF16)
        rows = jnp.dot(onehots[which], tokens, preferred_element_type=F32)
        for j, out in enumerate(outs[group * lay.experts : (group + 1) * lay.experts]):
            out[place, :, : lay.width] = rows[j * lay.main : (j + 1) * lay.main].astype(BF16)
            pack_extra(lay, rows, lay.experts * lay.main + j * lay.extra, out, place, stage)
    for copy in copies[2 + loads :]:
        copy.wait()


def opening(lay, chain, tables, items, groups, arrays, picks, limit):
    stack = jax.ShapeDtypeStruct((len(arrays), lay.tokens, lay.width), BF16)
    payloads = [
        jax.ShapeDtypeStruct((size, lay.main, lay.packed), BF16)
        for size in groups
        for _ in range(lay.experts)
    ]
    plan = tuple((which, scaled) for _, which, scaled in items)
    args = [tokens for tokens, _, _ in items] + list(tables) + list(arrays)
    outs = [stack] + payloads
    got = pl.pallas_call(
        functools.partial(opening_kernel, lay, plan, tuple(groups), tuple(picks)),
        out_shape=outs,
        in_specs=[HBM_SPEC] * len(args),
        out_specs=[VMEM_SPEC] * len(outs),
        scratch_shapes=[
            stage_shape(lay),
            pltpu.VMEM((len(items), lay.tokens, lay.width), BF16),
            pltpu.VMEM(tables[0].shape, jnp.int32),
            pltpu.VMEM(tables[1].shape, F32),
            pltpu.SemaphoreType.DMA((2 + len(items) + len(arrays),)),
        ],
        compiler_params=pltpu.CompilerParams(vmem_limit_bytes=limit * MIB),
        cost_estimate=cost(2 * lay.slots * lay.tokens * lay.width * len(items), args + outs),
    )(*args)
    chain.last = (got[1],)
    each = [got[1 + g * lay.experts : 1 + (g + 1) * lay.experts] for g in range(len(groups))]
    return got[0], each


def mirrored(value):
    count = lax.axis_size("section")
    return lax.ppermute(value, "section", [(i, count - 1 - i) for i in range(count)])


def passed_along(value, by):
    count = lax.axis_size("section")
    pairs = [(i, i + by) for i in range(count) if 0 <= i + by < count]
    return lax.ppermute(value, "section", pairs)


def per_device(
    left_in,
    left_new,
    left_saved,
    left_cot,
    right_in,
    right_saved,
    right_cot,
    right_cot_new,
    expert_ids,
    gate_values,
    w_gate,
    w_up,
    w_down,
):
    peers = lax.axis_size("expert")
    tokens, width = left_in.shape[1:]
    assert expert_ids.shape[-1] == 1
    lay = Layout(peers, tokens, width)
    slots = expert_ids.shape[0]
    tables = (
        expert_ids.reshape(2 * slots, 1, tokens),
        gate_values.reshape(2 * slots, 1, tokens),
    )
    f0, b0, f1, b1, f2, b2 = range(2 * slots)

    chain = Chain()
    weights = (w_gate[0, 0], w_up[0, 0], w_down[0, 0])
    left_first, cot_first, left_fresh, cot_fresh = left_in[0], left_cot[0], left_new, right_cot_new
    stack_zero, (sent_f0, sent_b1) = opening(
        lay,
        chain,
        tables,
        [(left_in[0], f0, False), (left_saved[0], b1, False), (left_cot[0], b1, True)],
        (1, 2),
        [right_saved, right_cot],
        [(0, 0), (0,)],
        56,
    )
    mirror_zero = mirrored(stack_zero)
    rows_f0 = dispatch(lay, sent_f0, True)
    rows_b1 = dispatch(lay, sent_b1, True)
    parts_f0, _ = run_experts(lay, chain, [("forward", (0, 0))], [rows_f0], weights)
    over_f0 = handed_over(lay, parts_f0, False)
    (sent_b0,) = route(
        lay,
        chain,
        tables,
        [(mirror_zero, 0, b0, False, None, None), (mirror_zero, 1, b0, True, None, None)],
        (2,),
    )
    rows_b0 = dispatch(lay, sent_b0, True)
    saved_two = mirrored(stacked(lay, chain, [right_saved], [(1, 0)]))
    back_f0 = summed(lay, chain, parts_f0, over_f0)
    parts_b1, (kept_b1,) = run_experts(
        lay, chain, [("backward", (0, 0), (0, 1))], [rows_b1], weights
    )
    over_b1 = handed_over(lay, parts_b1, True)
    left_zero = combine(lay, chain, tables, f0, True, left_first, back_f0, 0)
    arriving = passed_along(left_zero, 1)
    parts_b0, (kept_b0,) = run_experts(
        lay, chain, [("backward", (0, 0), (0, 1))], [rows_b0], weights
    )
    over_b0 = handed_over(lay, parts_b0, True)
    back_b0 = summed(lay, chain, parts_b0, over_b0)
    back_b1 = summed(lay, chain, parts_b1, over_b1)
    right_first = mirrored(stacked(lay, chain, [right_in], [(0,)]))
    (sent_f2,) = route(
        lay,
        chain,
        tables,
        [(saved_two, 0, b2, False, None, None), (arriving, None, f2, False, "first", left_fresh)],
        (2,),
    )
    rows_f2 = dispatch(lay, sent_f2, True)
    rows_s1, lead_f2 = rows_f2, 1
    back_zero = combine(lay, chain, tables, b0, False, mirror_zero, back_b0, 0, lead=1)
    returning = passed_along(back_zero, -1)
    back_one = combine(lay, chain, tables, b1, False, cot_first, back_b1, 0)
    (sent_f1,) = route(
        lay, chain, tables, [(right_first, 0, f1, False, None, None)], (1,)
    )
    rows_f1 = dispatch(lay, sent_f1, True)
    parts_f2, _ = run_experts(lay, chain, [("forward", (0, lead_f2))], [rows_f2], weights)
    over_f2 = handed_over(lay, parts_f2, True)
    (sent_c2,) = route(
        lay, chain, tables, [(returning, None, b2, True, "last", cot_fresh)], (1,)
    )
    cots_b2 = dispatch(lay, sent_c2, True)
    back_f2 = summed(lay, chain, parts_f2, over_f2)
    parts_f1, _ = run_experts(lay, chain, [("forward", (0, 0))], [rows_f1], weights)
    over_f1 = handed_over(lay, parts_f1, True)
    parts_b2, (kept_b2,) = run_experts(
        lay, chain, [("backward", (0, 0), (1, 0))], [rows_s1, cots_b2], weights
    )
    over_b2 = handed_over(lay, parts_b2, True)
    back_f1 = summed(lay, chain, parts_f1, over_f1)
    left_out = combine(
        lay,
        chain,
        tables,
        f2,
        True,
        arriving,
        back_f2,
        0,
        edge="first",
        fresh=left_fresh,
        first=left_zero,
    )
    grad_gate, grad_up, grad_down = all_gradients(chain, (kept_b0, kept_b1, kept_b2))
    back_b2 = summed(lay, chain, parts_b2, over_b2)
    right_out = combine(lay, chain, tables, f1, True, right_first, back_f1, 0, lead=0)
    right_back = combine(
        lay,
        chain,
        tables,
        b2,
        False,
        returning,
        back_b2,
        0,
        edge="last",
        fresh=cot_fresh,
        first=back_zero,
    )
    return (
        left_out[:, None],
        right_out[None],
        back_one[None],
        right_back[:, None],
        grad_gate[None, None],
        grad_up[None, None],
        grad_down[None, None],
    )


def solution(mesh):
    in_specs = (
        P("section", "expert", None),
        P("expert", None),
        P("section", "expert", None),
        P("section", "expert", None),
        P("section", "expert", None),
        P(None, "section", "expert", None),
        P("section", "expert", None),
        P("expert", None),
        P(None, None, "section", "expert", None),
        P(None, None, "section", "expert", None),
        P("section", "expert", None, None),
        P("section", "expert", None, None),
        P("section", "expert", None, None),
    )
    out_specs = (
        P(None, "section", "expert", None),
        P("section", "expert", None),
        P("section", "expert", None),
        P(None, "section", "expert", None),
        P("section", "expert", None, None),
        P("section", "expert", None, None),
        P("section", "expert", None, None),
    )
    return jax.shard_map(
        per_device, mesh=mesh, in_specs=in_specs, out_specs=out_specs, check_vma=False
    )
```

```python
import functools

import jax
import jax.numpy as jnp
from jax import lax
from jax.experimental import pallas as pl
from jax.experimental.pallas import tpu as pltpu
from jax.sharding import PartitionSpec as P

LANES = 128
F32 = jnp.float32
BF16 = jnp.bfloat16
MIB = 1024 * 1024


class Layout:
    def __init__(self, peers, tokens, width):
        self.peers = peers
        self.experts = peers // 2
        self.tokens = tokens
        self.width = width
        self.cap = min(tokens, 2 * ((tokens // self.experts + 1) // 2) + 2)
        self.main = self.cap // 8 * 8
        self.extra = self.cap - self.main
        self.slabs = width // LANES
        self.per_group = self.main // self.extra if self.extra else 1
        self.groups = -(-self.slabs // self.per_group) if self.extra else 0
        self.packed = width + self.groups * LANES
        self.slots = -(-(self.experts * self.cap) // 16) * 16
        self.rows = peers * self.cap
        self.rows_held = -(-self.rows // 16) * 16


def slab_place(lay, slab):
    group, at = divmod(slab, lay.per_group)
    return at * lay.extra, lay.width + group * LANES


def pack_extra(lay, rows, start, out_ref, lead, stage):
    if not lay.extra:
        return
    if lay.slabs % lay.per_group:
        stage[...] = jnp.zeros_like(stage)
    part = rows[start : start + lay.extra, :]
    for slab in range(lay.slabs):
        row, col = slab_place(lay, slab)
        stage[row : row + lay.extra, col - lay.width : col - lay.width + LANES] = part[
            :, slab * LANES : (slab + 1) * LANES
        ]
    out_ref[lead, :, lay.width :] = stage[...].astype(BF16)


def unpack_extra(lay, packed, stage, into, row_at):
    stage[...] = packed
    for slab in range(lay.slabs):
        row, col = slab_place(lay, slab)
        into[row_at : row_at + lay.extra, slab * LANES : (slab + 1) * LANES] = stage[
            row : row + lay.extra, col - lay.width : col - lay.width + LANES
        ]


def stacked_main(lay, blocks):
    if lay.main % 16:
        return jnp.concatenate([b.astype(F32) for b in blocks], axis=0).astype(BF16)
    return jnp.concatenate(blocks, axis=0)


def as_column(row):
    square = (row.shape[1], row.shape[1])
    down = lax.broadcasted_iota(jnp.int32, square, 0)
    across = lax.broadcasted_iota(jnp.int32, square, 1)
    return jnp.sum(jnp.where(down == across, row, jnp.zeros_like(row)), axis=1, keepdims=True)


def slot_onehot(lay, ids_row):
    tokens = lay.tokens
    own_expert = lax.axis_index("expert") // 2
    down = lax.broadcasted_iota(jnp.int32, (tokens, tokens), 0)
    across = lax.broadcasted_iota(jnp.int32, (tokens, tokens), 1)
    earlier = jnp.logical_and(as_column(ids_row) == ids_row, down < across)
    rank = jnp.sum(earlier.astype(jnp.int32), axis=0, keepdims=True)
    near = ids_row ^ own_expert
    slot = jnp.where(
        rank < lay.main,
        near * lay.main + rank,
        lay.experts * lay.main + near * lay.extra + rank - lay.main,
    )
    place = lax.broadcasted_iota(jnp.int32, (lay.slots, tokens), 0)
    return (place == slot).astype(F32).astype(BF16)


def stage_shape(lay):
    return pltpu.VMEM((lay.main, max(1, lay.groups) * LANES), F32)


def at_edge(edge):
    last = lax.axis_size("section") - 1
    return lax.axis_index("section") == (0 if edge == "first" else last)


def route_kernel(lay, plan, groups, loads, *refs):
    inputs = sum(1 if edge is None else 2 for *_, edge in plan)
    ids, gates = refs[inputs : inputs + 2]
    outs = refs[inputs + 2 : inputs + 2 + len(groups) * lay.experts]
    chosen = list(refs[inputs + 2 + len(outs) : inputs + 2 + len(outs) + inputs - len(plan)])
    scratch = refs[inputs + 2 + len(outs) + len(chosen) :]
    stage = scratch[0]
    copies = []
    for i in range(loads):
        copies.append(pltpu.make_async_copy(refs[i], scratch[1].at[i], scratch[2].at[i]))
        copies[-1].start()
    onehots = {which: slot_onehot(lay, ids[which]) for which, *_ in plan}

    def read(at, lead):
        if loads:
            copies[at].wait()
            return scratch[1][at]
        return refs[at][...] if lead is None else refs[at][lead]

    at = 0
    places = [(g, lead) for g, size in enumerate(groups) for lead in range(size)]
    for (group, place), (which, lead, scaled, edge) in zip(places, plan):
        tokens = read(at, lead)
        at += 1
        if edge is not None:
            tokens = jnp.where(at_edge(edge), read(at, None), tokens)
            at += 1
            chosen.pop(0)[...] = tokens
        if scaled:
            tokens = (as_column(gates[which]) * tokens.astype(F32)).astype(BF16)
        rows = jnp.dot(onehots[which], tokens, preferred_element_type=F32)
        for j in range(lay.experts):
            out = outs[group * lay.experts + j]
            out[place, :, : lay.width] = rows[j * lay.main : (j + 1) * lay.main].astype(BF16)
            pack_extra(lay, rows, lay.experts * lay.main + j * lay.extra, out, place, stage)


VMEM_SPEC = pl.BlockSpec(memory_space=pltpu.VMEM)
ANY_SPEC = pl.BlockSpec(memory_space=pl.ANY)
HBM_SPEC = pl.BlockSpec(memory_space=pltpu.HBM)


def cost(flops, arrays):
    moved = sum(a.size * a.dtype.itemsize for a in arrays)
    return pl.CostEstimate(flops=int(flops), bytes_accessed=int(moved), transcendentals=0)


class Chain:
    def __init__(self):
        self.last = ()


def call(chain, kernel, args, outs, scratch, flops, limit, in_hbm=0):
    after = chain.last
    specs = [HBM_SPEC] * in_hbm + [VMEM_SPEC] * (len(args) - in_hbm) + [ANY_SPEC] * len(after)

    def body(*refs):
        kernel(*refs[: len(args)], *refs[len(args) + len(after) :])

    got = pl.pallas_call(
        body,
        out_shape=outs,
        in_specs=specs,
        out_specs=[VMEM_SPEC] * len(outs),
        scratch_shapes=scratch,
        compiler_params=pltpu.CompilerParams(vmem_limit_bytes=limit * MIB),
        cost_estimate=cost(flops, list(args) + list(outs)),
    )(*args, *after)
    chain.last = (got[0],)
    return got


def route(lay, chain, tables, items, groups, in_hbm=False, limit=10):
    args = []
    plan = []
    for tokens, lead, which, scaled, edge, fresh in items:
        args.append(tokens)
        if fresh is not None:
            args.append(fresh)
        plan.append((which, lead, scaled, edge))
    loads = len(args) if in_hbm else 0
    outs = [
        jax.ShapeDtypeStruct((size, lay.main, lay.packed), BF16)
        for size in groups
        for _ in range(lay.experts)
    ]
    taken = jax.ShapeDtypeStruct((lay.tokens, lay.width), BF16)
    outs += [taken] * sum(edge is not None for *_, edge in plan)
    scratch = [stage_shape(lay)]
    if loads:
        scratch += [
            pltpu.VMEM((loads, lay.tokens, lay.width), BF16),
            pltpu.SemaphoreType.DMA((loads,)),
        ]
    got = call(
        chain,
        functools.partial(route_kernel, lay, tuple(plan), tuple(groups), loads),
        args + list(tables),
        outs,
        scratch,
        2 * lay.slots * lay.tokens * lay.width * len(items),
        limit,
        loads,
    )
    sent = [got[g * lay.experts : (g + 1) * lay.experts] for g in range(len(groups))]
    return sent + list(got[len(groups) * lay.experts :])


def stack_kernel(picks, *refs):
    count = len(picks)
    out, sems = refs[count], refs[count + 1]
    copies = []
    for at, pick in enumerate(picks):
        source = refs[at]
        for i in pick:
            source = source.at[i]
        copies.append(pltpu.make_async_copy(source, out.at[at], sems.at[at]))
    for copy in copies:
        copy.start()
    for copy in copies:
        copy.wait()


def stacked(lay, chain, arrays, picks, limit=4):
    count = len(arrays)
    out = jax.ShapeDtypeStruct((count, lay.tokens, lay.width), BF16)
    scratch = [pltpu.SemaphoreType.DMA((count,))]
    kernel = functools.partial(stack_kernel, tuple(picks))
    return call(chain, kernel, arrays, [out], scratch, 0, limit, count)[0]


def swapped(lay, value, bits):
    return lax.ppermute(value, "expert", [(i, i ^ bits) for i in range(lay.peers)])


def dispatch(lay, payloads, direct=False):
    got = []
    for j, payload in enumerate(payloads):
        here = payload if j == 0 else swapped(lay, payload, 2 * j)
        over = swapped(lay, payload, 2 * j + 1) if direct else swapped(lay, here, 1)
        got += [here, over]
    return got


def add_kernel(left, right, out):
    out[...] = (left[...].astype(F32) + right[...].astype(F32)).astype(BF16)


def handed_over(lay, parts, direct=False):
    if direct:
        return [parts[0]] + [swapped(lay, parts[d], d) for d in range(1, lay.peers)]
    return [swapped(lay, parts[2 * j + 1], 1) for j in range(lay.experts)]


def summed(lay, chain, parts, others):
    if len(others) == lay.peers:
        return others
    totals = []
    for j in range(1, lay.experts):
        other = others[j]
        out = jax.ShapeDtypeStruct(other.shape, BF16)
        total = call(chain, add_kernel, [parts[2 * j], other], [out], [], 2 * other.size, 4)[0]
        totals.append(swapped(lay, total, 2 * j))
    return [parts[0], others[0]] + totals


def load_rows(lay, refs, lead, stage, extra_rows):
    main = stacked_main(lay, [r[lead, :, : lay.width] for r in refs])
    if not lay.extra:
        return main
    extra_rows[...] = jnp.zeros_like(extra_rows)
    for d, ref in enumerate(refs):
        unpack_extra(lay, ref[lead, :, lay.width :].astype(F32), stage, extra_rows, d * lay.extra)
    return jnp.concatenate([main, extra_rows[...].astype(BF16)], axis=0)


def store_parts(lay, rows, refs, lead, stage):
    for d, ref in enumerate(refs):
        ref[lead, :, : lay.width] = rows[d * lay.main : (d + 1) * lay.main].astype(BF16)
        pack_extra(lay, rows, lay.peers * lay.main + d * lay.extra, ref, lead, stage)


def extra_shape(lay):
    return pltpu.VMEM((lay.rows_held - lay.peers * lay.main, lay.width), F32)


NT = (((1,), (1,)), ((), ()))
TN = (((0,), (0,)), ((), ()))


def expert_kernel(lay, tasks, groups, *refs):
    n = lay.peers
    blocks = [refs[g * n : (g + 1) * n] for g in range(groups)]
    at = groups * n
    w_gate, w_up, w_down = refs[at : at + 3]
    outs = refs[at + 3 : at + 3 + n]
    kept = refs[at + 3 + n : len(refs) - 2]
    stage, extra_rows = refs[len(refs) - 2 :]
    for task, (kind, *sources) in enumerate(tasks):
        held = [load_rows(lay, blocks[g], lead, stage, extra_rows) for g, lead in sources]
        rows = held[0]
        gate = jnp.dot(rows, w_gate[...], preferred_element_type=F32)
        up = jnp.dot(rows, w_up[...], preferred_element_type=F32)
        logistic = jax.nn.sigmoid(gate)
        swish = gate * logistic
        hidden = (swish * up).astype(BF16)
        if kind == "forward":
            part = jnp.dot(hidden, w_down[...], preferred_element_type=F32)
            store_parts(lay, part, outs, task, stage)
            continue
        row_cot = held[1]
        d_hidden = lax.dot_general(row_cot, w_down[...], NT, preferred_element_type=F32)
        d_gate = (d_hidden * up * logistic * (1.0 + gate * (1.0 - logistic))).astype(BF16)
        d_up = (d_hidden * swish).astype(BF16)
        back = lax.dot_general(d_gate, w_gate[...], NT, preferred_element_type=F32)
        back = back + lax.dot_general(d_up, w_up[...], NT, preferred_element_type=F32)
        store_parts(lay, back, outs, task, stage)
        rows_out, cot_out, both_out, hidden_out = kept[:4]
        kept = kept[4:]
        half = d_gate.shape[1]
        rows_out[...] = rows
        cot_out[...] = row_cot
        both_out[:, :half] = d_gate
        both_out[:, half:] = d_up
        hidden_out[...] = hidden


def run_experts(lay, chain, tasks, groups, weights):
    half = weights[0].shape[1]
    out = jax.ShapeDtypeStruct((len(tasks), lay.main, lay.packed), BF16)
    wide = jax.ShapeDtypeStruct((lay.rows_held, lay.width), BF16)
    both = jax.ShapeDtypeStruct((lay.rows_held, 2 * half), BF16)
    narrow = jax.ShapeDtypeStruct((lay.rows_held, half), BF16)
    backs = sum(task[0] == "backward" for task in tasks)
    products = 3 * (len(tasks) - backs) + 5 * backs
    got = call(
        chain,
        functools.partial(expert_kernel, lay, tuple(tasks), len(groups)),
        [block for group in groups for block in group] + list(weights),
        [out] * lay.peers + [wide, wide, both, narrow] * backs,
        [stage_shape(lay), extra_shape(lay)],
        2 * products * lay.rows * lay.width * half,
        20,
    )
    kept = got[lay.peers :]
    return got[: lay.peers], [tuple(kept[4 * i : 4 * i + 4]) for i in range(backs)]


def mixed_tokens(lay, tokens, parts, task, ids_row, gates_row, stage, extra_rows):
    pairs = [[parts[0], parts[1]]]
    if len(parts) == lay.peers:
        pairs += [[parts[2 * j], parts[2 * j + 1]] for j in range(1, lay.experts)]
    else:
        pairs += [[part] for part in parts[2:]]
    mains = []
    if lay.extra:
        extra_rows[...] = jnp.zeros_like(extra_rows)
    for j in range(lay.experts):
        total = functools.reduce(jnp.add, [part[task].astype(F32) for part in pairs[j]])
        mains.append(total[:, : lay.width].astype(BF16))
        if lay.extra:
            unpack_extra(lay, total[:, lay.width :], stage, extra_rows, j * lay.extra)
    outputs = stacked_main(lay, mains)
    if lay.slots > lay.experts * lay.main:
        outputs = jnp.concatenate([outputs, extra_rows[...].astype(BF16)], axis=0)
    onehot = slot_onehot(lay, ids_row)
    picked = lax.dot_general(onehot, outputs, TN, preferred_element_type=F32)
    if gates_row is not None:
        picked = picked * as_column(gates_row)
    return (tokens.astype(F32) + picked).astype(BF16)


def combine_kernel(lay, which, lead, scaled, edge, has_first, task, ids, gates, tokens_ref, *refs):
    at = 0
    tokens = tokens_ref[...] if lead is None else tokens_ref[lead]
    if edge is not None:
        tokens = jnp.where(at_edge(edge), refs[at][...], tokens)
        at += 1
    if has_first:
        first = refs[at]
        at += 1
    parts = refs[at : len(refs) - 3]
    out, stage, extra_rows = refs[len(refs) - 3 :]
    gates_row = gates[which] if scaled else None
    mixed = mixed_tokens(lay, tokens, parts, task, ids[which], gates_row, stage, extra_rows)
    if has_first:
        out[0] = first[...]
        out[1] = mixed
    else:
        out[...] = mixed


def combine(
    lay,
    chain,
    tables,
    which,
    scaled,
    tokens,
    parts,
    task,
    lead=None,
    edge=None,
    fresh=None,
    first=None,
):
    args = list(tables) + [tokens]
    if fresh is not None:
        args.append(fresh)
    if first is not None:
        args.append(first)
    args += list(parts)
    shape = (lay.tokens, lay.width)
    if first is not None:
        shape = (2,) + shape
    spare = max(8, lay.slots - lay.experts * lay.main)
    return call(
        chain,
        functools.partial(
            combine_kernel, lay, which, lead, scaled, edge, first is not None, task
        ),
        args,
        [jax.ShapeDtypeStruct(shape, BF16)],
        [stage_shape(lay), pltpu.VMEM((spare, lay.width), F32)],
        2 * lay.slots * lay.tokens * lay.width,
        8,
    )[0]


def all_gradients_kernel(passes, *refs):
    rows, cots, both, hidden = (
        jnp.concatenate([r[...] for r in refs[i * passes : (i + 1) * passes]], axis=0)
        for i in range(4)
    )
    grad_gate, grad_up, grad_down = refs[4 * passes :]
    half = hidden.shape[1]

    total = lax.dot_general(rows, both, TN, preferred_element_type=F32)
    grad_gate[...] = total[:, :half].astype(BF16)
    grad_up[...] = total[:, half:].astype(BF16)
    grad_down[...] = lax.dot_general(hidden, cots, TN, preferred_element_type=F32).astype(BF16)


def all_gradients(chain, kept):
    after = chain.last
    passes = len(kept)
    held, width = kept[0][0].shape
    half = kept[0][3].shape[1]
    tile = 8 * LANES if width % (8 * LANES) == 0 else width
    args = [k[i] for i in range(4) for k in kept]
    wide = pl.BlockSpec((held, tile), lambda i: (0, i))
    both = pl.BlockSpec((held, 2 * half), lambda i: (0, 0))
    narrow = pl.BlockSpec((held, half), lambda i: (0, 0))
    tall = pl.BlockSpec((tile, half), lambda i: (i, 0))
    flat = pl.BlockSpec((half, tile), lambda i: (0, i))
    outs = [
        jax.ShapeDtypeStruct((width, half), BF16),
        jax.ShapeDtypeStruct((width, half), BF16),
        jax.ShapeDtypeStruct((half, width), BF16),
    ]

    def body(*refs):
        all_gradients_kernel(passes, *refs[: len(args)], *refs[len(args) + len(after) :])

    return pl.pallas_call(
        body,
        grid=(width // tile,),
        out_shape=outs,
        in_specs=[wide] * (2 * passes) + [both] * passes + [narrow] * passes
        + [ANY_SPEC] * len(after),
        out_specs=[tall, tall, flat],
        compiler_params=pltpu.CompilerParams(vmem_limit_bytes=28 * MIB),
        cost_estimate=cost(2 * 3 * passes * held * width * half, args + outs),
    )(*args, *after)


def opening_kernel(lay, plan, groups, picks, *refs):
    loads, stacks = len(plan), len(picks)
    tokens_in, ids_in, gates_in = refs[:loads], refs[loads], refs[loads + 1]
    stacked_in = refs[loads + 2 : loads + 2 + stacks]
    stack_out = refs[loads + 2 + stacks]
    outs = refs[loads + 3 + stacks : loads + 3 + stacks + len(groups) * lay.experts]
    stage, held, ids, gates, sems = refs[loads + 3 + stacks + len(outs) :]
    places = [(g, lead) for g, size in enumerate(groups) for lead in range(size)]
    sources = []
    for at, pick in enumerate(picks):
        source = stacked_in[at]
        for i in pick:
            source = source.at[i]
        sources.append(source)
    copies = [
        pltpu.make_async_copy(ids_in, ids, sems.at[0]),
        pltpu.make_async_copy(gates_in, gates, sems.at[1]),
    ]
    copies += [
        pltpu.make_async_copy(tokens_in[i], held.at[i], sems.at[2 + i]) for i in range(loads)
    ]
    copies += [
        pltpu.make_async_copy(source, stack_out.at[at], sems.at[2 + loads + at])
        for at, source in enumerate(sources)
    ]
    for copy in copies:
        copy.start()
    copies[0].wait()
    copies[1].wait()
    onehots = {which: slot_onehot(lay, ids[which]) for which, _ in plan}
    for at, ((group, place), (which, scaled)) in enumerate(zip(places, plan)):
        copies[2 + at].wait()
        tokens = held[at]
        if scaled:
            tokens = (as_column(gates[which]) * tokens.astype(F32)).astype(BF16)
        rows = jnp.dot(onehots[which], tokens, preferred_element_type=F32)
        for j, out in enumerate(outs[group * lay.experts : (group + 1) * lay.experts]):
            out[place, :, : lay.width] = rows[j * lay.main : (j + 1) * lay.main].astype(BF16)
            pack_extra(lay, rows, lay.experts * lay.main + j * lay.extra, out, place, stage)
    for copy in copies[2 + loads :]:
        copy.wait()


def opening(lay, chain, tables, items, groups, arrays, picks, limit):
    stack = jax.ShapeDtypeStruct((len(arrays), lay.tokens, lay.width), BF16)
    payloads = [
        jax.ShapeDtypeStruct((size, lay.main, lay.packed), BF16)
        for size in groups
        for _ in range(lay.experts)
    ]
    plan = tuple((which, scaled) for _, which, scaled in items)
    args = [tokens for tokens, _, _ in items] + list(tables) + list(arrays)
    outs = [stack] + payloads
    got = pl.pallas_call(
        functools.partial(opening_kernel, lay, plan, tuple(groups), tuple(picks)),
        out_shape=outs,
        in_specs=[HBM_SPEC] * len(args),
        out_specs=[VMEM_SPEC] * len(outs),
        scratch_shapes=[
            stage_shape(lay),
            pltpu.VMEM((len(items), lay.tokens, lay.width), BF16),
            pltpu.VMEM(tables[0].shape, jnp.int32),
            pltpu.VMEM(tables[1].shape, F32),
            pltpu.SemaphoreType.DMA((2 + len(items) + len(arrays),)),
        ],
        compiler_params=pltpu.CompilerParams(vmem_limit_bytes=limit * MIB),
        cost_estimate=cost(2 * lay.slots * lay.tokens * lay.width * len(items), args + outs),
    )(*args)
    chain.last = (got[1],)
    each = [got[1 + g * lay.experts : 1 + (g + 1) * lay.experts] for g in range(len(groups))]
    return got[0], each


def mirrored(value):
    count = lax.axis_size("section")
    return lax.ppermute(value, "section", [(i, count - 1 - i) for i in range(count)])


def passed_along(value, by):
    count = lax.axis_size("section")
    pairs = [(i, i + by) for i in range(count) if 0 <= i + by < count]
    return lax.ppermute(value, "section", pairs)


def per_device(
    left_in,
    left_new,
    left_saved,
    left_cot,
    right_in,
    right_saved,
    right_cot,
    right_cot_new,
    expert_ids,
    gate_values,
    w_gate,
    w_up,
    w_down,
):
    peers = lax.axis_size("expert")
    tokens, width = left_in.shape[1:]
    assert expert_ids.shape[-1] == 1
    lay = Layout(peers, tokens, width)
    slots = expert_ids.shape[0]
    tables = (
        expert_ids.reshape(2 * slots, 1, tokens),
        gate_values.reshape(2 * slots, 1, tokens),
    )
    f0, b0, f1, b1, f2, b2 = range(2 * slots)

    chain = Chain()
    weights = (w_gate[0, 0], w_up[0, 0], w_down[0, 0])
    left_first, cot_first, left_fresh, cot_fresh = left_in[0], left_cot[0], left_new, right_cot_new
    stack_zero, (sent_f0, sent_b1) = opening(
        lay,
        chain,
        tables,
        [(left_in[0], f0, False), (left_saved[0], b1, False), (left_cot[0], b1, True)],
        (1, 2),
        [right_saved, right_cot],
        [(0, 0), (0,)],
        56,
    )
    mirror_zero = mirrored(stack_zero)
    rows_f0 = dispatch(lay, sent_f0, True)
    rows_b1 = dispatch(lay, sent_b1, True)
    parts_f0, _ = run_experts(lay, chain, [("forward", (0, 0))], [rows_f0], weights)
    over_f0 = handed_over(lay, parts_f0, False)
    (sent_b0,) = route(
        lay,
        chain,
        tables,
        [(mirror_zero, 0, b0, False, None, None), (mirror_zero, 1, b0, True, None, None)],
        (2,),
    )
    rows_b0 = dispatch(lay, sent_b0, True)
    saved_two = mirrored(stacked(lay, chain, [right_saved], [(1, 0)]))
    back_f0 = summed(lay, chain, parts_f0, over_f0)
    parts_b1, (kept_b1,) = run_experts(
        lay, chain, [("backward", (0, 0), (0, 1))], [rows_b1], weights
    )
    over_b1 = handed_over(lay, parts_b1, True)
    left_zero = combine(lay, chain, tables, f0, True, left_first, back_f0, 0)
    arriving = passed_along(left_zero, 1)
    parts_b0, (kept_b0,) = run_experts(
        lay, Chain(), [("backward", (0, 0), (0, 1))], [rows_b0], weights
    )
    over_b0 = handed_over(lay, parts_b0, True)
    back_b0 = summed(lay, chain, parts_b0, over_b0)
    back_b1 = summed(lay, chain, parts_b1, over_b1)
    right_first = mirrored(stacked(lay, chain, [right_in], [(0,)]))
    sent_f2, tokens_f2 = route(
        lay,
        chain,
        tables,
        [(saved_two, 0, b2, False, None, None), (arriving, None, f2, False, "first", left_fresh)],
        (2,),
    )
    rows_f2 = dispatch(lay, sent_f2, True)
    rows_s1, lead_f2 = rows_f2, 1
    back_zero = combine(lay, Chain(), tables, b0, False, mirror_zero, back_b0, 0, lead=1)
    returning = passed_along(back_zero, -1)
    back_one = combine(lay, chain, tables, b1, False, cot_first, back_b1, 0)
    (sent_f1,) = route(
        lay, chain, tables, [(right_first, 0, f1, False, None, None)], (1,)
    )
    rows_f1 = dispatch(lay, sent_f1, True)
    parts_f2, _ = run_experts(lay, chain, [("forward", (0, lead_f2))], [rows_f2], weights)
    over_f2 = handed_over(lay, parts_f2, True)
    sent_c2, tokens_c2 = route(
        lay, chain, tables, [(returning, None, b2, True, "last", cot_fresh)], (1,)
    )
    cots_b2 = dispatch(lay, sent_c2, True)
    back_f2 = summed(lay, chain, parts_f2, over_f2)
    parts_f1, _ = run_experts(lay, chain, [("forward", (0, 0))], [rows_f1], weights)
    over_f1 = handed_over(lay, parts_f1, True)
    parts_b2, (kept_b2,) = run_experts(
        lay, chain, [("backward", (0, 0), (1, 0))], [rows_s1, cots_b2], weights
    )
    over_b2 = handed_over(lay, parts_b2, True)
    back_f1 = summed(lay, chain, parts_f1, over_f1)
    left_out = combine(
        lay,
        Chain(),
        tables,
        f2,
        True,
        tokens_f2,
        back_f2,
        0,
        first=left_zero,
    )
    grad_gate, grad_up, grad_down = all_gradients(chain, (kept_b0, kept_b1, kept_b2))
    back_b2 = summed(lay, chain, parts_b2, over_b2)
    right_out = combine(lay, chain, tables, f1, True, right_first, back_f1, 0, lead=0)
    right_back = combine(
        lay,
        chain,
        tables,
        b2,
        False,
        tokens_c2,
        back_b2,
        0,
        first=back_zero,
    )
    return (
        left_out[:, None],
        right_out[None],
        back_one[None],
        right_back[:, None],
        grad_gate[None, None],
        grad_up[None, None],
        grad_down[None, None],
    )


def solution(mesh):
    in_specs = (
        P("section", "expert", None),
        P("expert", None),
        P("section", "expert", None),
        P("section", "expert", None),
        P("section", "expert", None),
        P(None, "section", "expert", None),
        P("section", "expert", None),
        P("expert", None),
        P(None, None, "section", "expert", None),
        P(None, None, "section", "expert", None),
        P("section", "expert", None, None),
        P("section", "expert", None, None),
        P("section", "expert", None, None),
    )
    out_specs = (
        P(None, "section", "expert", None),
        P("section", "expert", None),
        P("section", "expert", None),
        P(None, "section", "expert", None),
        P("section", "expert", None, None),
        P("section", "expert", None, None),
        P("section", "expert", None, None),
    )
    return jax.shard_map(
        per_device, mesh=mesh, in_specs=in_specs, out_specs=out_specs, check_vma=False
    )
```
